512 devices in a mesh: row: 32 (over y, z_hi, core), col: 16 (over x, z_lo).
Axes of the slice: x: 4, y: 4, z: 16 (z_hi: 4, z_lo: 4; z = z_hi * 4 + z_lo), core: 2. Of those that a mesh axis runs over, the one named last changes fastest.
Arguments:
- panels: bfloat16 [32768, 16384], P('row', 'col'), may hold values from -6 to 6
- self_factors: bfloat16 [4, 32768, 128], P(None, 'row'), may hold values from -0.375 to 0.375
- partner_factors: bfloat16 [4, 32768, 128], P(None, 'row'), may hold values from -0.375 to 0.375
- link_mask: int32 [4, 256], P(None, 'row'), may hold values 0 or 1
- block_ranks: int32 [256], P('row'), may hold values from 64 to 128, as said below
Outputs:
- coefficients: float32 [32768, 128], P('row')
The draws below stay inside these ranges and needn't reach their ends.
Inputs may be any that keep to these rules, and one draw needn't show every extreme that they name: `block_ranks`: number of leading basis rows used by each row block; both ends occur in every draw.
All inputs are finite; a program needn't handle non-finite values. No bound on the sum of `link_mask` on one device may be relied on, other than what follows from the above.
Results may differ from the reference program's by a relative error of at most 0.0012.
Values may be sent and summed in bfloat16 or wider, within the bound.
No kernel may reach another device: no remote copies, remote signals or barrier semaphores. Data moves between devices by JAX's collectives and lax.ppermute only.
A program may use at most 64 MiB of HBM per device.

```python
import math
import jax
import jax.numpy as jnp
from jax import lax

RANK = 128
BLOCKS = 8
P_DEV = 1024
LEVELS = 4
ROW_BLOCKS = 256
ROWS = 32768
COLUMNS = 16384
N_ROW = 32
N_COL = 16


def draw_block_ranks(key, part):
    key = jax.random.fold_in(key, 7)
    first_key, second_key = jax.random.split(key)
    values = jax.random.randint(first_key, (ROW_BLOCKS,), RANK // 2, RANK + 1)
    shuffled = jax.random.permutation(second_key, ROW_BLOCKS)
    values = values.at[shuffled[0]].set(RANK)
    values = values.at[shuffled[1]].set(RANK // 2)
    return values.astype(jnp.int32)


def with_ends(values, stream_key, least, high):
    shape = values.shape
    index_at = [jax.random.randint(jax.random.fold_in(stream_key, axis), (), 0, shape[axis]) for axis in range(len(shape))]
    values = values.at[tuple(index_at)].set(least)
    longest = shape.index(max(shape))
    index_at[longest] = (index_at[longest] + 1) % shape[longest]
    return values.at[tuple(index_at)].set(high)


def level_of(stream_key, extent, cuts, low, largest):
    gain = 1.0
    for dim, shards_of in cuts:
        steps = jax.random.uniform(jax.random.fold_in(jax.random.fold_in(stream_key, 6), dim), (shards_of,), jnp.float32, low / len(cuts), largest / len(cuts))
        gain = gain * jnp.repeat(jnp.exp(steps), extent[dim] // shards_of).reshape((-1,) + (1,) * (len(extent) - 1 - dim))
    return gain


def normal_values(stream_key, dims, spread, bound, pieces=(), held_as=jnp.bfloat16):
    loudness = level_of(stream_key, dims, pieces, -0.22, 0.18) if pieces else 1.0
    values = jax.random.normal(stream_key, dims, jnp.float32) * spread * loudness
    return jnp.minimum(jnp.maximum(values, -bound), bound).astype(held_as)


def setup_inputs(seed: int = 0) -> dict:
    splits = jax.random.split(jax.random.key(seed), 6)
    return {
        "panels": normal_values(splits[0], (ROWS, COLUMNS), 1.0, 6.0, ((0, 32), (1, 16))),
        "self_factors": normal_values(splits[1], (LEVELS, ROWS, RANK), (2 * RANK) ** -0.5, 0.375, ((1, 32),)),
        "partner_factors": normal_values(splits[2], (LEVELS, ROWS, RANK), (2 * RANK) ** -0.5, 0.375, ((1, 32),)),
        "link_mask": with_ends((jax.random.randint(splits[3], (LEVELS, ROW_BLOCKS), 0, 4) < 3).astype(jnp.int32), jax.random.fold_in(splits[3], 1), 0, 1),
        "block_ranks": draw_block_ranks(jax.random.fold_in(splits[5], 71), 0),
    }


def partner_order(bit_level):
    devices = jnp.arange(N_ROW, dtype=jnp.int32)
    partners = jnp.bitwise_xor(devices, 1 << bit_level)
    return (partners[:, None] * BLOCKS + jnp.arange(BLOCKS, dtype=jnp.int32)[None, :]).reshape(-1)

def settle(cross_sum, gram_sum, block_ranks):
    kept_mask = (jnp.arange(RANK, dtype=jnp.int32)[None, :] < block_ranks[:, None]).astype(jnp.float32)
    cross_sum = cross_sum * kept_mask[:, None, :]
    identity = jnp.eye(RANK, dtype=jnp.float32)
    gram_sum = gram_sum * kept_mask[:, :, None] * kept_mask[:, None, :] + identity * (1.0 - kept_mask)[:, None, :]
    cholesky_factor = jnp.linalg.cholesky(gram_sum)
    halfway = lax.linalg.triangular_solve(cholesky_factor, cross_sum, left_side=False, lower=True, transpose_a=True)
    result = lax.linalg.triangular_solve(cholesky_factor, halfway, left_side=False, lower=True, transpose_a=False)
    return 4.0 * math.sqrt(RANK) * result.reshape(-1, RANK)

def reference(panels, self_factors, partner_factors, link_mask, block_ranks):
    top_precision = lax.Precision.HIGHEST
    log_rows = N_ROW.bit_length() - 1
    level_bits = [(2 * tree_depth + 1) % log_rows for tree_depth in range(LEVELS)]
    blocks_all = N_ROW * BLOCKS
    own_blocks = self_factors.reshape(LEVELS, blocks_all, RANK, RANK).astype(jnp.float32)
    paired_blocks = partner_factors.reshape(LEVELS, blocks_all, RANK, RANK).astype(jnp.float32)
    coupling_weight = link_mask.astype(jnp.float32)

    def group_step(totals, col_start):
        cross_sum, gram_sum = totals
        random_projection = lax.dynamic_slice_in_dim(panels, col_start, P_DEV, 1)
        random_projection = random_projection.reshape(blocks_all, RANK, P_DEV).astype(jnp.float32)
        present_level = random_projection
        for tree_depth in range(LEVELS - 1):
            paired_index = present_level[partner_order(level_bits[tree_depth])]
            blended_rows = jnp.einsum('nrf,nfe->nre', own_blocks[tree_depth], present_level, precision=top_precision)
            blended_rows = blended_rows + coupling_weight[tree_depth][:, None, None] * jnp.einsum('nrf,nfe->nre', paired_blocks[tree_depth], paired_index, precision=top_precision)
            rounded = lax.optimization_barrier(blended_rows.astype(jnp.bfloat16))
            present_level = rounded.astype(jnp.float32)
        paired_index = present_level[partner_order(level_bits[-1])]
        inner_adjacent = jnp.einsum('hni,hei->hne', present_level, random_projection, precision=top_precision)
        inner_distant = jnp.einsum('hni,hei->hne', paired_index, random_projection, precision=top_precision)
        part_cross = jnp.einsum('gab,gbc->gac', own_blocks[-1], inner_adjacent, precision=top_precision)
        part_cross = part_cross + coupling_weight[-1][:, None, None] * jnp.einsum('gab,gbc->gac', paired_blocks[-1], inner_distant, precision=top_precision)
        partial_gram = jnp.einsum('hni,hei->hne', random_projection, random_projection, precision=top_precision)
        return ((cross_sum + part_cross, gram_sum + partial_gram), None)
    col_starts = jnp.arange(N_COL, dtype=jnp.int32) * P_DEV
    empty_sums = jnp.zeros((blocks_all, RANK, RANK), jnp.float32)
    (cross_sum, gram_sum), _ = lax.scan(group_step, (empty_sums, empty_sums), col_starts)
    return settle(cross_sum, gram_sum, block_ranks)
```

```python
import functools
import math

import jax
import jax.numpy as jnp
from jax import lax
from jax.experimental import pallas as pl
from jax.experimental.pallas import tpu as pltpu
from jax.sharding import Mesh, PartitionSpec as P

RANK = 128
LEVELS = 4
SLOTS = 8
ROW = ("yh", "yl", "zh", "core")
COL = ("x", "zl")
PEERS = ("yl", "zh")
HIGHEST = lax.Precision.HIGHEST


def invert_kernel(gram_ref, keep_ref, out_ref):
    lane = lax.broadcasted_iota(jnp.int32, (8, RANK), 1)
    sub = lax.broadcasted_iota(jnp.int32, (8, RANK), 0)
    rows = lax.broadcasted_iota(jnp.int32, (RANK, RANK), 0)
    cols = lax.broadcasted_iota(jnp.int32, (RANK, RANK), 1)
    blocks = gram_ref.shape[0]
    tiles = []
    for b in range(blocks):
        tiles.append([gram_ref[b, 8 * g : 8 * g + 8, :] for g in range(RANK // 8)])
    for k in range(RANK):
        first, at = k // 8, k % 8
        for b in range(blocks):
            tile = tiles[b]
            row = tile[first][at : at + 1, :]
            scaled = jnp.where(lane[:1] == k, 1.0, row) / row[:, k : k + 1]
            for g in range(first, RANK // 8):
                column = tile[g][:, k : k + 1]
                clear = lane == k
                if g == first:
                    column = jnp.where(sub[:, :1] > at, column, 0.0)
                    clear = clear & (sub > at)
                tile[g] = jnp.where(clear, 0.0, tile[g]) - column * scaled
    for b in range(blocks):
        done = jnp.concatenate(tiles[b], axis=0)
        pivots = jnp.sum(jnp.where(rows == cols, done, 0.0), axis=1, keepdims=True)
        lower = jnp.where(rows > cols, done, jnp.where(rows == cols, 1.0, 0.0))
        inverse = lax.dot_general(
            lower,
            lower / pivots,
            (((0,), (0,)), ((), ())),
            precision=HIGHEST,
            preferred_element_type=jnp.float32,
        )
        out_ref[b] = inverse * keep_ref[b] * (4.0 * math.sqrt(RANK))


def invert(gram, keep):
    return pl.pallas_call(
        invert_kernel,
        out_shape=jax.ShapeDtypeStruct(gram.shape, jnp.float32),
        in_specs=[pl.BlockSpec(memory_space=pltpu.VMEM)] * 2,
        out_specs=pl.BlockSpec(memory_space=pltpu.VMEM),
        compiler_params=pltpu.CompilerParams(vmem_limit_bytes=32 * 2**20),
    )(gram, jnp.broadcast_to(keep[:, :, None], gram.shape))


def pick(blocks, index):
    return lax.dynamic_index_in_dim(blocks, index, 0, keepdims=False)


def body(panels, self_factors, partner_factors, link_mask, block_ranks):
    local_cols = panels.shape[1]
    me = lax.axis_index("yl") * 4 + lax.axis_index("zh")
    x_at, zl_at = lax.axis_index("x"), lax.axis_index("zl")
    own = panels.reshape(SLOTS, RANK, local_cols)

    base = [pick(own, me)]
    for r in range(1, SLOTS):
        base.append(
            lax.ppermute(pick(own, me ^ r), PEERS, [(i, i ^ r) for i in range(SLOTS)])
        )

    quarter = RANK // 4
    start = x_at, 0, zl_at * quarter, 0
    shape = 1, SLOTS, quarter, RANK
    mask = lax.dynamic_index_in_dim(link_mask, x_at, 0, keepdims=False).astype(jnp.bfloat16)
    own_rows = lax.dynamic_slice(
        self_factors.reshape(LEVELS, SLOTS, RANK, RANK), start, shape
    )[0]
    paired_rows = lax.dynamic_slice(
        partner_factors.reshape(LEVELS, SLOTS, RANK, RANK), start, shape
    )[0]
    pair = jnp.concatenate([own_rows, paired_rows * mask[:, None, None]], axis=2)
    pair = lax.all_to_all(pair, PEERS, 0, 0, tiled=True)
    pair = jnp.stack([pick(pair, me ^ r) for r in range(SLOTS)])
    pair = lax.all_gather(pair, "zl", axis=1, tiled=True)
    factors = lax.all_gather(pair, "x", axis=0)

    gram = jnp.einsum("hni,hei->hne", own, own, preferred_element_type=jnp.float32)
    gram = lax.all_to_all(gram.reshape(4, 2, RANK, RANK), "x", 0, 0, tiled=True).sum(0)
    gram = lax.all_gather(gram, "zl", axis=0).sum(0)
    ranks = lax.dynamic_slice_in_dim(block_ranks, x_at * 2, 2, 0)
    keep = (jnp.arange(RANK, dtype=jnp.int32)[None, :] < ranks[:, None]).astype(jnp.float32)
    identity = jnp.eye(RANK, dtype=jnp.float32)
    gram = gram * keep[:, :, None] * keep[:, None, :] + identity * (1.0 - keep)[:, None, :]
    inverse = lax.all_gather(invert(gram, keep), "x", axis=0, tiled=True)

    base = jnp.stack(base)
    flip = lambda level, bit: jnp.stack([level[r ^ bit] for r in range(SLOTS)])
    mix = lambda depth, level, paired: jnp.einsum(
        "hnf,hfe->hne",
        factors[depth],
        jnp.concatenate([level, paired], axis=1),
        preferred_element_type=jnp.float32,
    ).astype(jnp.bfloat16)
    level = mix(0, base, flip(base, 1))
    level = mix(1, level, flip(level, 4))
    level = mix(2, level, lax.ppermute(level, "core", [(0, 1), (1, 0)]))
    dots = functools.partial(jnp.einsum, "hni,hei->hne", preferred_element_type=jnp.float32)
    near = dots(level, base)
    far = dots(flip(level, 2), base)
    cross = jnp.einsum(
        "gab,gbc->gac",
        factors[3].astype(jnp.float32),
        jnp.concatenate([near, far], axis=1),
        precision=HIGHEST,
    )

    cross = cross.reshape(SLOTS, 16, 8, RANK).transpose(1, 0, 2, 3)
    cross = lax.all_to_all(cross, COL, 0, 0, tiled=True).sum(0)
    cross = jnp.stack([pick(cross, me ^ r) for r in range(SLOTS)])
    cross = lax.all_to_all(cross, PEERS, 0, 0, tiled=True)
    solved = jnp.einsum("jrk,jkm->jrm", cross, inverse, precision=HIGHEST)
    solved = jnp.broadcast_to(solved[None], (16,) + solved.shape)
    solved = lax.all_to_all(solved, COL, 0, 0, tiled=True)
    return solved.transpose(1, 0, 2, 3).reshape(-1, RANK)


def solution(mesh):
    split = Mesh(mesh.devices.reshape(2, 2, 4, 2, 4, 4), ROW + COL)
    return jax.shard_map(
        body,
        mesh=split,
        in_specs=(P(ROW, COL), P(None, ROW, None), P(None, ROW, None), P(None, ROW), P(ROW)),
        out_specs=P(ROW, None),
        check_vma=False,
    )
```

```python
import math

import jax
import jax.numpy as jnp
from jax import lax
from jax.experimental import pallas as pl
from jax.experimental.pallas import tpu as pltpu
from jax.sharding import Mesh, PartitionSpec as P

RANK = 128
LEVELS = 4
SLOTS = 8
ROW = ("yh", "yl", "zh", "core")
COL = ("x", "zl")
PEERS = ("yl", "zh")
HIGHEST = lax.Precision.HIGHEST


def gram_kernel(panels_ref, out_ref):
    rows = lax.broadcasted_iota(jnp.int32, (RANK, RANK), 0)
    cols = lax.broadcasted_iota(jnp.int32, (RANK, RANK), 1)

    def gram(block):
        value = panels_ref[block * RANK : (block + 1) * RANK]
        return lax.dot_general(
            value, value, (((1,), (1,)), ((), ())), preferred_element_type=jnp.float32
        )

    for pair in range(out_ref.shape[0]):
        below, above = gram(2 * pair), gram(2 * pair + 1)
        out_ref[pair, :RANK] = jnp.where(rows >= cols, below, above)
        diagonal = jnp.sum(jnp.where(rows == cols, above, 0.0), axis=0, keepdims=True)
        out_ref[pair, RANK:] = jnp.broadcast_to(diagonal, (8, RANK))


def local_grams(panels):
    return pl.pallas_call(
        gram_kernel,
        out_shape=jax.ShapeDtypeStruct((SLOTS // 2, RANK + 8, RANK), jnp.float32),
        in_specs=[pl.BlockSpec(memory_space=pltpu.VMEM)],
        out_specs=pl.BlockSpec(memory_space=pltpu.VMEM),
        compiler_params=pltpu.CompilerParams(vmem_limit_bytes=32 * 2**20),
    )(panels)


def invert_kernel(place_ref, ranks_ref, packed_ref, out_ref):
    lane = lax.broadcasted_iota(jnp.int32, (8, RANK), 1)
    sub = lax.broadcasted_iota(jnp.int32, (8, RANK), 0)
    rows = lax.broadcasted_iota(jnp.int32, (RANK, RANK), 0)
    cols = lax.broadcasted_iota(jnp.int32, (RANK, RANK), 1)
    blocks = out_ref.shape[0]
    packed = packed_ref[0, :RANK]
    turned = packed.T
    above = jnp.where(rows < cols, packed, turned)
    grams = (
        jnp.where(rows >= cols, packed, turned),
        jnp.where(rows == cols, packed_ref[0, RANK : RANK + 1], above),
    )
    ranks = [ranks_ref[place_ref[0] * blocks + b] for b in range(blocks)]
    tiles = []
    for b in range(blocks):
        kept = (rows < ranks[b]) & (cols < ranks[b])
        gram = jnp.where(kept, grams[b], jnp.where(rows == cols, 1.0, 0.0))
        tiles.append([gram[8 * g : 8 * g + 8] for g in range(RANK // 8)])
    for k in range(RANK):
        first, at = k // 8, k % 8
        for b in range(blocks):
            tile = tiles[b]
            row = tile[first][at : at + 1, :]
            scaled = jnp.where(lane[:1] == k, 1.0, row) / row[:, k : k + 1]
            for g in range(first, RANK // 8):
                column = tile[g][:, k : k + 1]
                clear = lane == k
                if g == first:
                    column = jnp.where(sub[:, :1] > at, column, 0.0)
                    clear = clear & (sub > at)
                tile[g] = jnp.where(clear, 0.0, tile[g]) - column * scaled
    for b in range(blocks):
        done = jnp.concatenate(tiles[b], axis=0)
        pivots = jnp.sum(jnp.where(rows == cols, done, 0.0), axis=1, keepdims=True)
        lower = jnp.where(rows > cols, done, jnp.where(rows == cols, 1.0, 0.0))
        inverse = lax.dot_general(
            lower,
            lower / pivots,
            (((0,), (0,)), ((), ())),
            precision=HIGHEST,
            preferred_element_type=jnp.float32,
        )
        out_ref[b] = jnp.where(rows < ranks[b], inverse * (4.0 * math.sqrt(RANK)), 0.0)


def invert(place, block_ranks, packed):
    smem = pl.BlockSpec(memory_space=pltpu.SMEM)
    return pl.pallas_call(
        invert_kernel,
        out_shape=jax.ShapeDtypeStruct((2, RANK, RANK), jnp.float32),
        in_specs=[smem, smem, pl.BlockSpec(memory_space=pltpu.VMEM)],
        out_specs=pl.BlockSpec(memory_space=pltpu.VMEM),
        compiler_params=pltpu.CompilerParams(vmem_limit_bytes=32 * 2**20),
    )(place, block_ranks, packed)


def factor_of(factors_ref, place_ref, level, slot, flipped=False):
    factor = factors_ref[(level + 4 - place_ref[0]) % 4, slot]
    if flipped:
        factor = jnp.concatenate([factor[:, RANK:], factor[:, :RANK]], axis=1)
    return factor


def joint(factors_ref, place_ref, level, slot, other):
    return jnp.concatenate(
        [
            factor_of(factors_ref, place_ref, level, slot),
            factor_of(factors_ref, place_ref, level, other, True),
        ],
        axis=0,
    )


def matmul(left, right):
    return jnp.dot(left, right, preferred_element_type=jnp.float32)


def near_levels_kernel(place_ref, base_ref, factors_ref, *rest):
    out_ref, mid_ref = rest[-2:]
    columns = out_ref.shape[2]
    for source, target, level, bit in ((base_ref, mid_ref, 0, 1), (mid_ref, out_ref, 1, 4)):
        for slot in range(SLOTS):
            other = slot ^ bit
            if slot < other:
                rows = jnp.concatenate([source[slot, :, :columns], source[other, :, :columns]], axis=0)
                mixed = matmul(joint(factors_ref, place_ref, level, slot, other), rows)
                mixed = mixed.astype(jnp.bfloat16)
                target[slot] = mixed[:RANK]
                target[other] = mixed[RANK:]


def near_levels(place, base, factors, columns, *after):
    vmem = pl.BlockSpec(memory_space=pltpu.VMEM)
    smem = pl.BlockSpec(memory_space=pltpu.SMEM)
    shape = SLOTS, RANK, columns
    return pl.pallas_call(
        near_levels_kernel,
        out_shape=jax.ShapeDtypeStruct(shape, base.dtype),
        in_specs=[smem, vmem, vmem] + [pl.BlockSpec(memory_space=pl.ANY)] * len(after),
        out_specs=vmem,
        scratch_shapes=[pltpu.VMEM(shape, base.dtype)],
        compiler_params=pltpu.CompilerParams(vmem_limit_bytes=32 * 2**20),
    )(place, base, factors, *after)


def sums_of(place_ref, factors_ref, level_ref, paired_ref, base_ref, slot, other):
    def third(at):
        rows = jnp.concatenate([level_ref[at], paired_ref[at]], axis=0)
        return matmul(factor_of(factors_ref, place_ref, 2, at), rows).astype(jnp.bfloat16)

    columns = level_ref.shape[2]
    rows = jnp.concatenate([third(slot), third(other)], axis=0)
    bases = jnp.concatenate([base_ref[slot, :, :columns], base_ref[other, :, :columns]], axis=0)
    return lax.dot_general(
        rows, bases, (((1,), (1,)), ((), ())), preferred_element_type=jnp.float32
    )


PAIRS = tuple((slot, slot ^ 2) for slot in range(SLOTS) if slot < slot ^ 2)


def early_kernel(place_ref, factors_ref, level_ref, paired_ref, base_ref, out_ref):
    for at, (slot, other) in enumerate(PAIRS):
        out_ref[at] = sums_of(
            place_ref, factors_ref, level_ref, paired_ref, base_ref, slot, other
        )


def cross_kernel(place_ref, factors_ref, level_ref, paired_ref, base_ref, early_ref, out_ref):
    for at, (slot, other) in enumerate(PAIRS):
        sums = early_ref[at] + sums_of(
            place_ref, factors_ref, level_ref, paired_ref, base_ref, slot, other
        )
        parts = []
        for _ in range(3):
            part = sums.astype(jnp.bfloat16)
            parts.append(part)
            sums = sums - part.astype(jnp.float32)
        factor = (
            factor_of(factors_ref, place_ref, 3, slot),
            factor_of(factors_ref, place_ref, 3, other, True),
        )
        for side, block in enumerate((slot, other)):
            side_of = slice(side * RANK, (side + 1) * RANK)
            cross = sum(matmul(factor[side], part[:, side_of]) for part in parts[::-1])
            for x in range(4):
                for zl in range(4):
                    start = 8 * (4 * x + zl)
                    out_ref[x, block, zl] = cross[start : start + 8]


def sums_call(kernel, shape, place, *arrays):
    vmem = pl.BlockSpec(memory_space=pltpu.VMEM)
    return pl.pallas_call(
        kernel,
        out_shape=jax.ShapeDtypeStruct(shape, jnp.float32),
        in_specs=[pl.BlockSpec(memory_space=pltpu.SMEM)] + [vmem] * len(arrays),
        out_specs=vmem,
        compiler_params=pltpu.CompilerParams(vmem_limit_bytes=32 * 2**20),
    )(place, *arrays)


def nothing_kernel(*refs):
    del refs


def once_done(value, *others):
    return pl.pallas_call(
        nothing_kernel,
        out_shape=jax.ShapeDtypeStruct(value.shape, value.dtype),
        in_specs=[pl.BlockSpec(memory_space=pl.ANY)] * (1 + len(others)),
        out_specs=pl.BlockSpec(memory_space=pl.ANY),
        input_output_aliases={0: 0},
    )(value, *others)


def exchange(blocks, axes):
    return lax.all_to_all(blocks, axes, 0, 0, tiled=True)


def gather(block, axes):
    count = lax.axis_size(axes)
    return exchange(jnp.broadcast_to(block[None], (count,) + block.shape), axes)


def swap(block, axis, bit):
    return lax.ppermute(block, axis, [(i, i ^ bit) for i in range(lax.axis_size(axis))])


def along_x(block, *after):
    count = lax.axis_size("x")
    shift = lambda d: lax.ppermute(block, "x", [(i, (i - d) % count) for i in range(count)])
    own = once_done(block, *after) if after else block
    return jnp.stack([own] + [shift(d) for d in range(1, count)])


def part(blocks, at, count):
    return lax.dynamic_slice_in_dim(blocks, at * count, count, 0)


def grams(panels):
    x_at = lax.axis_index("x")
    packed = local_grams(panels)
    high, low = x_at // 2, x_at % 2
    packed = part(packed, high, 2) + swap(part(packed, 1 - high, 2), "x", 2)
    packed = part(packed, low, 1) + swap(part(packed, 1 - low, 1), "x", 1)
    return packed + swap(packed, "zl", 1) + (swap(packed, "zl", 2) + swap(packed, "zl", 3))


def to_every_x(inverse):
    x_at = lax.axis_index("x")
    every = along_x(inverse)
    order = [lax.dynamic_index_in_dim(every, (x + 4 - x_at) % 4, 0, False) for x in range(4)]
    return jnp.concatenate(order, axis=0)


def gather_halved(solved):
    top = jnp.max(jnp.abs(solved), axis=2)
    power = jnp.clip(jnp.floor(jnp.log2(jnp.maximum(top, 1e-36))), -120.0, 120.0)
    values = (solved * jnp.exp2(-power)[:, :, None]).astype(jnp.float16)
    powers = jnp.pad(power.astype(jnp.float16), ((0, 0), (0, RANK - power.shape[1])))
    sent = gather(jnp.concatenate([values, powers[None]], axis=0), COL)
    blocks = solved.shape[0]
    power = sent[:, blocks, :, : solved.shape[1]].astype(jnp.float32)
    values = sent[:, :blocks].astype(jnp.float32) * jnp.exp2(power)[:, :, :, None]
    return values.transpose(1, 0, 2, 3).reshape(-1, RANK)


def first_kernel(place_ref, mask_ref, panels_ref, own_ref, paired_ref, out_ref):
    columns = panels_ref.shape[1]
    for slot in range(SLOTS):
        rows = slice(slot * RANK, (slot + 1) * RANK)
        mask = mask_ref[place_ref[0], slot].astype(jnp.float32)
        out_ref[slot, :, :columns] = panels_ref[rows]
        out_ref[slot, :, columns : columns + RANK] = own_ref[0, rows]
        paired = paired_ref[0, rows].astype(jnp.float32) * mask
        out_ref[slot, :, columns + RANK :] = paired.astype(jnp.bfloat16)


def first_part(place, panels, self_factors, partner_factors, link_mask, columns):
    rows = panels.shape[0]
    level = pl.BlockSpec((1, rows, RANK), lambda i, place: (place[0], 0, 0))
    shape = SLOTS, RANK, columns + 2 * RANK
    return pl.pallas_call(
        first_kernel,
        out_shape=jax.ShapeDtypeStruct(shape, panels.dtype),
        grid_spec=pltpu.PrefetchScalarGridSpec(
            num_scalar_prefetch=1,
            grid=(1,),
            in_specs=[
                pl.BlockSpec(memory_space=pltpu.SMEM),
                pl.BlockSpec((rows, columns), lambda i, place: (0, 0)),
                level,
                level,
            ],
            out_specs=pl.BlockSpec(shape, lambda i, place: (0, 0, 0)),
        ),
        compiler_params=pltpu.CompilerParams(vmem_limit_bytes=60 * 2**20),
    )(place, link_mask, panels, self_factors, partner_factors)


def body(panels, self_factors, partner_factors, link_mask, block_ranks):
    columns = panels.shape[1]
    early = columns // 2
    late = columns - early
    own = panels.reshape(SLOTS, RANK, columns)
    place = lax.axis_index("x").astype(jnp.int32).reshape(1)

    first = first_part(place, panels, self_factors, partner_factors, link_mask, early)
    first = exchange(first, PEERS)
    gram = grams(panels)
    second = exchange(once_done(own[:, :, early:], first, gram), PEERS)
    inverse = invert(place, block_ranks, gram)
    factors = along_x(first[:, :, early:], inverse)
    inverse = to_every_x(inverse)

    level = near_levels(place, first, factors, early)
    paired = swap(level, "core", 1)
    sums = sums_call(
        early_kernel, (len(PAIRS), 2 * RANK, 2 * RANK), place, factors, level, paired, first
    )
    level = near_levels(place, second, factors, late, inverse, sums)
    paired = swap(level, "core", 1)
    cross = sums_call(
        cross_kernel, (4, SLOTS, 4, 8, RANK), place, factors, level, paired, second, sums
    )

    cross = exchange(cross.reshape(4, 4 * SLOTS, 8, RANK), "x").sum(0)
    cross = exchange(cross, PEERS + ("zl",)).reshape(SLOTS, 4, 8, RANK).sum(1)
    solved = jnp.einsum("jrk,jkm->jrm", cross, inverse, precision=HIGHEST)
    return gather_halved(solved)


def solution(mesh):
    split = Mesh(mesh.devices.reshape(2, 2, 4, 2, 4, 4), ROW + COL)
    return jax.shard_map(
        body,
        mesh=split,
        in_specs=(P(ROW, COL), P(None, ROW, None), P(None, ROW, None), P(None, ROW), P(ROW)),
        out_specs=P(ROW, None),
        check_vma=False,
    )
```

```python
import math

import jax
import jax.numpy as jnp
from jax import lax
from jax.experimental import pallas as pl
from jax.experimental.pallas import tpu as pltpu
from jax.sharding import Mesh, PartitionSpec as P

RANK = 128
LEVELS = 4
SLOTS = 8
ROW = ("yh", "yl", "zh", "core")
COL = ("x", "zl")
PEERS = ("yl", "zh")
HIGHEST = lax.Precision.HIGHEST


def gram_kernel(panels_ref, out_ref):
    rows = lax.broadcasted_iota(jnp.int32, (RANK, RANK), 0)
    cols = lax.broadcasted_iota(jnp.int32, (RANK, RANK), 1)

    def gram(block):
        value = panels_ref[block * RANK : (block + 1) * RANK]
        return lax.dot_general(
            value, value, (((1,), (1,)), ((), ())), preferred_element_type=jnp.float32
        )

    for pair in range(out_ref.shape[0]):
        below, above = gram(2 * pair), gram(2 * pair + 1)
        out_ref[pair, :RANK] = jnp.where(rows >= cols, below, above)
        diagonal = jnp.sum(jnp.where(rows == cols, above, 0.0), axis=0, keepdims=True)
        out_ref[pair, RANK:] = jnp.broadcast_to(diagonal, (8, RANK))


def local_grams(panels):
    return pl.pallas_call(
        gram_kernel,
        out_shape=jax.ShapeDtypeStruct((SLOTS // 2, RANK + 8, RANK), jnp.float32),
        in_specs=[pl.BlockSpec(memory_space=pltpu.VMEM)],
        out_specs=pl.BlockSpec(memory_space=pltpu.VMEM),
        compiler_params=pltpu.CompilerParams(vmem_limit_bytes=16 * 2**20),
    )(panels)


def invert_kernel(place_ref, ranks_ref, packed_ref, out_ref):
    lane = lax.broadcasted_iota(jnp.int32, (8, RANK), 1)
    sub = lax.broadcasted_iota(jnp.int32, (8, RANK), 0)
    rows = lax.broadcasted_iota(jnp.int32, (RANK, RANK), 0)
    cols = lax.broadcasted_iota(jnp.int32, (RANK, RANK), 1)
    blocks = out_ref.shape[0]
    packed = packed_ref[0, :RANK]
    turned = packed.T
    above = jnp.where(rows < cols, packed, turned)
    grams = (
        jnp.where(rows >= cols, packed, turned),
        jnp.where(rows == cols, packed_ref[0, RANK : RANK + 1], above),
    )
    ranks = [ranks_ref[place_ref[0] * blocks + b] for b in range(blocks)]
    tiles = []
    for b in range(blocks):
        kept = (rows < ranks[b]) & (cols < ranks[b])
        gram = jnp.where(kept, grams[b], jnp.where(rows == cols, 1.0, 0.0))
        tiles.append([gram[8 * g : 8 * g + 8] for g in range(RANK // 8)])
    for k in range(RANK):
        first, at = k // 8, k % 8
        for b in range(blocks):
            tile = tiles[b]
            row = tile[first][at : at + 1, :]
            scaled = jnp.where(lane[:1] == k, 1.0, row) / row[:, k : k + 1]
            for g in range(first, RANK // 8):
                column = tile[g][:, k : k + 1]
                clear = lane == k
                if g == first:
                    column = jnp.where(sub[:, :1] > at, column, 0.0)
                    clear = clear & (sub > at)
                tile[g] = jnp.where(clear, 0.0, tile[g]) - column * scaled
    for b in range(blocks):
        done = jnp.concatenate(tiles[b], axis=0)
        pivots = jnp.sum(jnp.where(rows == cols, done, 0.0), axis=1, keepdims=True)
        lower = jnp.where(rows > cols, done, jnp.where(rows == cols, 1.0, 0.0))
        inverse = lax.dot_general(
            lower,
            lower / pivots,
            (((0,), (0,)), ((), ())),
            precision=HIGHEST,
            preferred_element_type=jnp.float32,
        )
        out_ref[b] = jnp.where(rows < ranks[b], inverse * (4.0 * math.sqrt(RANK)), 0.0)


def invert(place, block_ranks, packed):
    smem = pl.BlockSpec(memory_space=pltpu.SMEM)
    return pl.pallas_call(
        invert_kernel,
        out_shape=jax.ShapeDtypeStruct((2, RANK, RANK), jnp.float32),
        in_specs=[smem, smem, pl.BlockSpec(memory_space=pltpu.VMEM)],
        out_specs=pl.BlockSpec(memory_space=pltpu.VMEM),
        compiler_params=pltpu.CompilerParams(vmem_limit_bytes=16 * 2**20),
    )(place, block_ranks, packed)


def factor_of(factors_ref, level, slot, flipped=False):
    factor = factors_ref[level % 2, slot]
    if flipped:
        factor = jnp.concatenate([factor[:, RANK:], factor[:, :RANK]], axis=1)
    return factor


def joint(factors_ref, level, slot, other):
    return jnp.concatenate(
        [
            factor_of(factors_ref, level, slot),
            factor_of(factors_ref, level, other, True),
        ],
        axis=0,
    )


def matmul(left, right):
    return jnp.dot(left, right, preferred_element_type=jnp.float32)


def near_levels_kernel(base_ref, factors_ref, *rest):
    out_ref, mid_ref = rest[-2:]
    columns = out_ref.shape[2]
    for source, target, level, bit in ((base_ref, mid_ref, 0, 1), (mid_ref, out_ref, 1, 4)):
        for slot in range(SLOTS):
            other = slot ^ bit
            if slot < other:
                rows = jnp.concatenate([source[slot, :, :columns], source[other, :, :columns]], axis=0)
                mixed = matmul(joint(factors_ref, level, slot, other), rows)
                mixed = mixed.astype(jnp.bfloat16)
                target[slot] = mixed[:RANK]
                target[other] = mixed[RANK:]


def near_levels(base, factors, columns, *after):
    vmem = pl.BlockSpec(memory_space=pltpu.VMEM)
    shape = SLOTS, RANK, columns
    return pl.pallas_call(
        near_levels_kernel,
        out_shape=jax.ShapeDtypeStruct(shape, base.dtype),
        in_specs=[vmem, vmem] + [pl.BlockSpec(memory_space=pl.ANY)] * len(after),
        out_specs=vmem,
        scratch_shapes=[pltpu.VMEM(shape, base.dtype)],
        compiler_params=pltpu.CompilerParams(vmem_limit_bytes=16 * 2**20),
    )(base, factors, *[corner(other) for other in after])


def sums_of(factors_ref, level_ref, paired_ref, base_ref, slot, other):
    def third(at):
        rows = jnp.concatenate([level_ref[at], paired_ref[at]], axis=0)
        return matmul(factor_of(factors_ref, 2, at), rows).astype(jnp.bfloat16)

    columns = level_ref.shape[2]
    rows = jnp.concatenate([third(slot), third(other)], axis=0)
    bases = jnp.concatenate([base_ref[slot, :, :columns], base_ref[other, :, :columns]], axis=0)
    return lax.dot_general(
        rows, bases, (((1,), (1,)), ((), ())), preferred_element_type=jnp.float32
    )


PAIRS = tuple((slot, slot ^ 2) for slot in range(SLOTS) if slot < slot ^ 2)


def early_kernel(factors_ref, level_ref, paired_ref, base_ref, out_ref):
    for at, (slot, other) in enumerate(PAIRS):
        out_ref[at] = sums_of(
            factors_ref, level_ref, paired_ref, base_ref, slot, other
        )


def cross_kernel(factors_ref, level_ref, paired_ref, base_ref, early_ref, out_ref):
    for at, (slot, other) in enumerate(PAIRS):
        sums = early_ref[at] + sums_of(
            factors_ref, level_ref, paired_ref, base_ref, slot, other
        )
        parts = []
        for _ in range(3):
            part = sums.astype(jnp.bfloat16)
            parts.append(part)
            sums = sums - part.astype(jnp.float32)
        factor = (
            factor_of(factors_ref, 3, slot),
            factor_of(factors_ref, 3, other, True),
        )
        for side, block in enumerate((slot, other)):
            side_of = slice(side * RANK, (side + 1) * RANK)
            cross = sum(matmul(factor[side], part[:, side_of]) for part in parts[::-1])
            for x in range(4):
                for zl in range(4):
                    start = 8 * (4 * x + zl)
                    out_ref[block // 4, x, block % 4, zl] = cross[start : start + 8]


def sums_call(kernel, shape, *arrays):
    vmem = pl.BlockSpec(memory_space=pltpu.VMEM)
    return pl.pallas_call(
        kernel,
        out_shape=jax.ShapeDtypeStruct(shape, jnp.float32),
        in_specs=[vmem] * len(arrays),
        out_specs=vmem,
        compiler_params=pltpu.CompilerParams(vmem_limit_bytes=16 * 2**20),
    )(*arrays)


def nothing_kernel(*refs):
    del refs


def corner(value):
    value = value.reshape(-1, *value.shape[-2:])
    return value[0, :16, :RANK]


def once_done(value, *others):
    others = [corner(other) for other in others]
    return pl.pallas_call(
        nothing_kernel,
        out_shape=jax.ShapeDtypeStruct(value.shape, value.dtype),
        in_specs=[pl.BlockSpec(memory_space=pl.ANY)] * (1 + len(others)),
        out_specs=pl.BlockSpec(memory_space=pl.ANY),
        input_output_aliases={0: 0},
    )(value, *others)


def exchange(blocks, axes):
    return lax.all_to_all(blocks, axes, 0, 0, tiled=True)


def gather(block, axes):
    count = lax.axis_size(axes)
    return exchange(jnp.broadcast_to(block[None], (count,) + block.shape), axes)


def swap(block, axis, bit):
    return lax.ppermute(block, axis, [(i, i ^ bit) for i in range(lax.axis_size(axis))])


def along_x(block, *after):
    count = lax.axis_size("x")
    shift = lambda d: lax.ppermute(block, "x", [(i, (i - d) % count) for i in range(count)])
    own = once_done(block, *after) if after else block
    return jnp.stack([own] + [shift(d) for d in range(1, count)])


def part(blocks, at, count):
    return lax.dynamic_slice_in_dim(blocks, at * count, count, 0)


def grams(panels):
    x_at = lax.axis_index("x")
    packed = local_grams(panels)
    high, low = x_at // 2, x_at % 2
    packed = part(packed, high, 2) + swap(part(packed, 1 - high, 2), "x", 2)
    packed = part(packed, low, 1) + swap(part(packed, 1 - low, 1), "x", 1)
    return packed + swap(packed, "zl", 1) + (swap(packed, "zl", 2) + swap(packed, "zl", 3))


def by_place(every):
    x_at = lax.axis_index("x")
    return [lax.dynamic_index_in_dim(every, (x + 4 - x_at) % 4, 0, False) for x in range(4)]


def gather_halved(solved):
    top = jnp.max(jnp.abs(solved), axis=2)
    power = jnp.clip(jnp.floor(jnp.log2(jnp.maximum(top, 1e-36))), -120.0, 120.0)
    values = (solved * jnp.exp2(-power)[:, :, None]).astype(jnp.float16)
    powers = jnp.pad(power.astype(jnp.float16), ((0, 0), (0, RANK - power.shape[1])))
    sent = gather(jnp.concatenate([values, powers[None]], axis=0), COL)
    blocks = solved.shape[0]
    power = sent[:, blocks, :, : solved.shape[1]].astype(jnp.float32)
    values = sent[:, :blocks].astype(jnp.float32) * jnp.exp2(power)[:, :, :, None]
    return values.transpose(1, 0, 2, 3).reshape(-1, RANK)


def first_kernel(place_ref, mask_ref, panels_ref, own_ref, paired_ref, out_ref):
    columns = panels_ref.shape[1]
    for slot in range(SLOTS):
        rows = slice(slot * RANK, (slot + 1) * RANK)
        mask = mask_ref[place_ref[0], slot].astype(jnp.float32)
        out_ref[slot, :, :columns] = panels_ref[rows]
        out_ref[slot, :, columns : columns + RANK] = own_ref[0, rows]
        paired = paired_ref[0, rows].astype(jnp.float32) * mask
        out_ref[slot, :, columns + RANK :] = paired.astype(jnp.bfloat16)


def first_part(place, panels, self_factors, partner_factors, link_mask, columns):
    rows = panels.shape[0]
    level = pl.BlockSpec((1, rows, RANK), lambda i, place: (place[0], 0, 0))
    shape = SLOTS, RANK, columns + 2 * RANK
    return pl.pallas_call(
        first_kernel,
        out_shape=jax.ShapeDtypeStruct(shape, panels.dtype),
        grid_spec=pltpu.PrefetchScalarGridSpec(
            num_scalar_prefetch=1,
            grid=(1,),
            in_specs=[
                pl.BlockSpec(memory_space=pltpu.SMEM),
                pl.BlockSpec((rows, columns), lambda i, place: (0, 0)),
                level,
                level,
            ],
            out_specs=pl.BlockSpec(shape, lambda i, place: (0, 0, 0)),
        ),
        compiler_params=pltpu.CompilerParams(vmem_limit_bytes=60 * 2**20),
    )(place, link_mask, panels, self_factors, partner_factors)


def body(panels, self_factors, partner_factors, link_mask, block_ranks):
    columns = panels.shape[1]
    early = columns * 3 // 8
    late = columns - early
    own = panels.reshape(SLOTS, RANK, columns)
    place = lax.axis_index("x").astype(jnp.int32).reshape(1)

    first = first_part(place, panels, self_factors, partner_factors, link_mask, early)
    first = exchange(first, PEERS)
    gram = grams(panels)
    second = exchange(once_done(own[:, :, early:], first, gram), PEERS)
    inverse = invert(place, block_ranks, gram)
    factors = along_x(first[:, :, early:], inverse)
    inverse = along_x(once_done(inverse, factors))
    factors = by_place(factors)
    lower, upper = jnp.stack(factors[:2]), jnp.stack(factors[2:])

    level = near_levels(first, lower, early)
    paired = swap(level, "core", 1)
    shape = len(PAIRS), 2 * RANK, 2 * RANK
    sums = sums_call(early_kernel, shape, upper, level, paired, first)
    level = near_levels(second, lower, late, sums, inverse)
    paired = swap(level, "core", 1)
    shape = 2, 4, 4, 4, 8, RANK
    cross = sums_call(cross_kernel, shape, upper, level, paired, second, sums)

    cross = exchange(cross.reshape(2 * 4, 16, 8, RANK), ("yl", "x"))
    cross = cross.reshape(2, 4, 16, 8, RANK).sum(1)
    cross = exchange(cross.transpose(1, 0, 2, 3), ("zh", "zl"))
    cross = cross.reshape(4, 4, 2, 8, RANK).sum(1)
    cross = cross.transpose(1, 0, 2, 3).reshape(SLOTS, 8, RANK)
    inverse = jnp.concatenate(by_place(inverse), axis=0)
    solved = jnp.einsum("jrk,jkm->jrm", cross, inverse, precision=HIGHEST)
    return gather_halved(solved)


def solution(mesh):
    split = Mesh(mesh.devices.reshape(2, 2, 4, 2, 4, 4), ROW + COL)
    return jax.shard_map(
        body,
        mesh=split,
        in_specs=(P(ROW, COL), P(None, ROW, None), P(None, ROW, None), P(None, ROW), P(ROW)),
        out_specs=P(ROW, None),
        check_vma=False,
    )
```

```python
import math

import jax
import jax.numpy as jnp
from jax import lax
from jax.experimental import pallas as pl
from jax.experimental.pallas import tpu as pltpu
from jax.sharding import Mesh, PartitionSpec as P

RANK = 128
LEVELS = 4
SLOTS = 8
ROW = ("yh", "yl", "zh", "core")
COL = ("x", "zl")
PEERS = ("yl", "zh")
HIGHEST = lax.Precision.HIGHEST


def gram_kernel(panels_ref, out_ref, copy_ref):
    rows = lax.broadcasted_iota(jnp.int32, (RANK, RANK), 0)
    cols = lax.broadcasted_iota(jnp.int32, (RANK, RANK), 1)

    def gram(block):
        value = panels_ref[block * RANK : (block + 1) * RANK]
        return lax.dot_general(
            value, value, (((1,), (1,)), ((), ())), preferred_element_type=jnp.float32
        )

    for pair in range(out_ref.shape[0]):
        below, above = gram(2 * pair), gram(2 * pair + 1)
        out_ref[pair, :RANK] = jnp.where(rows >= cols, below, above)
        diagonal = jnp.sum(jnp.where(rows == cols, above, 0.0), axis=0, keepdims=True)
        out_ref[pair, RANK:] = jnp.broadcast_to(diagonal, (8, RANK))
    copy_ref[...] = panels_ref[...]


def local_grams(panels):
    return pl.pallas_call(
        gram_kernel,
        out_shape=(
            jax.ShapeDtypeStruct((SLOTS // 2, RANK + 8, RANK), jnp.float32),
            jax.ShapeDtypeStruct(panels.shape, panels.dtype),
        ),
        in_specs=[pl.BlockSpec(memory_space=pltpu.VMEM)],
        out_specs=[pl.BlockSpec(memory_space=pltpu.VMEM)] * 2,
        compiler_params=pltpu.CompilerParams(vmem_limit_bytes=16 * 2**20),
    )(panels)


def invert_kernel(place_ref, ranks_ref, packed_ref, out_ref):
    lane = lax.broadcasted_iota(jnp.int32, (8, RANK), 1)
    sub = lax.broadcasted_iota(jnp.int32, (8, RANK), 0)
    rows = lax.broadcasted_iota(jnp.int32, (RANK, RANK), 0)
    cols = lax.broadcasted_iota(jnp.int32, (RANK, RANK), 1)
    blocks = out_ref.shape[0]
    packed = packed_ref[0, :RANK]
    turned = packed.T
    above = jnp.where(rows < cols, packed, turned)
    grams = (
        jnp.where(rows >= cols, packed, turned),
        jnp.where(rows == cols, packed_ref[0, RANK : RANK + 1], above),
    )
    ranks = [ranks_ref[place_ref[0] * blocks + b] for b in range(blocks)]
    tiles = []
    for b in range(blocks):
        kept = (rows < ranks[b]) & (cols < ranks[b])
        gram = jnp.where(kept, grams[b], jnp.where(rows == cols, 1.0, 0.0))
        tiles.append([gram[8 * g : 8 * g + 8] for g in range(RANK // 8)])
    for k in range(RANK):
        first, at = k // 8, k % 8
        for b in range(blocks):
            tile = tiles[b]
            row = tile[first][at : at + 1, :]
            scaled = jnp.where(lane[:1] == k, 1.0, row) / row[:, k : k + 1]
            for g in range(first, RANK // 8):
                column = tile[g][:, k : k + 1]
                clear = lane == k
                if g == first:
                    column = jnp.where(sub[:, :1] > at, column, 0.0)
                    clear = clear & (sub > at)
                tile[g] = jnp.where(clear, 0.0, tile[g]) - column * scaled
    for b in range(blocks):
        done = jnp.concatenate(tiles[b], axis=0)
        pivots = jnp.sum(jnp.where(rows == cols, done, 0.0), axis=1, keepdims=True)
        lower = jnp.where(rows > cols, done, jnp.where(rows == cols, 1.0, 0.0))
        inverse = lax.dot_general(
            lower,
            lower / pivots,
            (((0,), (0,)), ((), ())),
            precision=HIGHEST,
            preferred_element_type=jnp.float32,
        )
        out_ref[b] = jnp.where(rows < ranks[b], inverse * (4.0 * math.sqrt(RANK)), 0.0)


def invert(place, block_ranks, packed):
    smem = pl.BlockSpec(memory_space=pltpu.SMEM)
    return pl.pallas_call(
        invert_kernel,
        out_shape=jax.ShapeDtypeStruct((2, RANK, RANK), jnp.float32),
        in_specs=[smem, smem, pl.BlockSpec(memory_space=pltpu.VMEM)],
        out_specs=pl.BlockSpec(memory_space=pltpu.VMEM),
        compiler_params=pltpu.CompilerParams(vmem_limit_bytes=16 * 2**20),
    )(place, block_ranks, packed)


def factor_of(factors_ref, level, slot, flipped=False):
    factor = factors_ref[level % 2, slot]
    if flipped:
        factor = jnp.concatenate([factor[:, RANK:], factor[:, :RANK]], axis=1)
    return factor


def joint(factors_ref, level, slot, other):
    return jnp.concatenate(
        [
            factor_of(factors_ref, level, slot),
            factor_of(factors_ref, level, other, True),
        ],
        axis=0,
    )


def matmul(left, right):
    return jnp.dot(left, right, preferred_element_type=jnp.float32)


def near_levels_kernel(base_ref, factors_ref, *rest):
    out_ref, mid_ref = rest[-2:]
    columns = out_ref.shape[2]
    for source, target, level, bit in ((base_ref, mid_ref, 0, 1), (mid_ref, out_ref, 1, 4)):
        for slot in range(SLOTS):
            other = slot ^ bit
            if slot < other:
                rows = jnp.concatenate([source[slot, :, :columns], source[other, :, :columns]], axis=0)
                mixed = matmul(joint(factors_ref, level, slot, other), rows)
                mixed = mixed.astype(jnp.bfloat16)
                target[slot] = mixed[:RANK]
                target[other] = mixed[RANK:]


def near_levels(base, factors, columns, *after):
    vmem = pl.BlockSpec(memory_space=pltpu.VMEM)
    shape = SLOTS, RANK, columns
    return pl.pallas_call(
        near_levels_kernel,
        out_shape=jax.ShapeDtypeStruct(shape, base.dtype),
        in_specs=[vmem, vmem] + [pl.BlockSpec(memory_space=pl.ANY)] * len(after),
        out_specs=vmem,
        scratch_shapes=[pltpu.VMEM(shape, base.dtype)],
        compiler_params=pltpu.CompilerParams(vmem_limit_bytes=16 * 2**20),
    )(base, factors, *[corner(other) for other in after])


def sums_of(factors_ref, level_ref, paired_ref, base_ref, slot, other):
    def third(at):
        rows = jnp.concatenate([level_ref[at], paired_ref[at]], axis=0)
        return matmul(factor_of(factors_ref, 2, at), rows).astype(jnp.bfloat16)

    columns = level_ref.shape[2]
    rows = jnp.concatenate([third(slot), third(other)], axis=0)
    bases = jnp.concatenate([base_ref[slot, :, :columns], base_ref[other, :, :columns]], axis=0)
    return lax.dot_general(
        rows, bases, (((1,), (1,)), ((), ())), preferred_element_type=jnp.float32
    )


PAIRS = tuple((slot, slot ^ 2) for slot in range(SLOTS) if slot < slot ^ 2)


def cross_kernel(factors_ref, level_ref, paired_ref, base_ref, out_ref):
    for slot, other in PAIRS:
        sums = sums_of(factors_ref, level_ref, paired_ref, base_ref, slot, other)
        parts = []
        for _ in range(3):
            part = sums.astype(jnp.bfloat16)
            parts.append(part)
            sums = sums - part.astype(jnp.float32)
        factor = (
            factor_of(factors_ref, 3, slot),
            factor_of(factors_ref, 3, other, True),
        )
        for side, block in enumerate((slot, other)):
            side_of = slice(side * RANK, (side + 1) * RANK)
            cross = sum(matmul(factor[side], part[:, side_of]) for part in parts[::-1])
            for x in range(4):
                out_ref[block // 4, x, block % 4] = cross[32 * x : 32 * x + 32]


def sums_call(kernel, shape, *arrays):
    vmem = pl.BlockSpec(memory_space=pltpu.VMEM)
    return pl.pallas_call(
        kernel,
        out_shape=jax.ShapeDtypeStruct(shape, jnp.float32),
        in_specs=[vmem] * len(arrays),
        out_specs=vmem,
        compiler_params=pltpu.CompilerParams(vmem_limit_bytes=16 * 2**20),
    )(*arrays)


def nothing_kernel(*refs):
    del refs


def corner(value):
    value = value.reshape(-1, *value.shape[-2:])
    return value[0, :16, :RANK]


def once_done(value, *others):
    others = [corner(other) for other in others]
    return pl.pallas_call(
        nothing_kernel,
        out_shape=jax.ShapeDtypeStruct(value.shape, value.dtype),
        in_specs=[pl.BlockSpec(memory_space=pl.ANY)] * (1 + len(others)),
        out_specs=pl.BlockSpec(memory_space=pl.ANY),
        input_output_aliases={0: 0},
    )(value, *others)


def exchange(blocks, axes):
    return lax.all_to_all(blocks, axes, 0, 0, tiled=True)


def gather(block, axes):
    count = lax.axis_size(axes)
    return exchange(jnp.broadcast_to(block[None], (count,) + block.shape), axes)


def swap(block, axis, bit):
    return lax.ppermute(block, axis, [(i, i ^ bit) for i in range(lax.axis_size(axis))])


def along_x(block, *after):
    count = lax.axis_size("x")
    shift = lambda d: lax.ppermute(block, "x", [(i, (i - d) % count) for i in range(count)])
    own = once_done(block, *after) if after else block
    return jnp.stack([own] + [shift(d) for d in range(1, count)])


def part(blocks, at, count):
    return lax.dynamic_slice_in_dim(blocks, at * count, count, 0)


def grams(panels):
    zl_at = lax.axis_index("zl")
    packed, panels = local_grams(panels)
    total = part(packed, zl_at, 1)
    for other in range(1, 4):
        total = total + swap(part(packed, zl_at ^ other, 1), "zl", other)
    return total, panels


def by_place(every):
    x_at = lax.axis_index("x")
    return [lax.dynamic_index_in_dim(every, (x + 4 - x_at) % 4, 0, False) for x in range(4)]


def gather_halved(solved):
    blocks, rows, _ = solved.shape
    top = jnp.max(jnp.abs(solved), axis=2)
    power = jnp.clip(jnp.floor(jnp.log2(jnp.maximum(top, 1e-36))), -120.0, 120.0)
    values = (solved * jnp.exp2(-power)[:, :, None]).astype(jnp.float16)
    powers = jnp.pad(power.T.astype(jnp.float16), ((0, 0), (0, RANK - blocks)))
    sent = gather(jnp.concatenate([values, powers[None]], axis=0), COL)
    power = sent[:, blocks, :, :blocks].astype(jnp.float32).transpose(0, 2, 1)
    values = sent[:, :blocks].astype(jnp.float32) * jnp.exp2(power)[:, :, :, None]
    values = values.reshape(4, 2, 2, blocks, rows, RANK)
    return values.transpose(1, 3, 0, 2, 4, 5).reshape(-1, RANK)


def level_kernel(place_ref, mask_ref, own_ref, paired_ref, out_ref):
    for slot in range(SLOTS):
        mask = mask_ref[place_ref[0], slot].astype(jnp.float32)
        out_ref[slot, :, :RANK] = own_ref[0, slot, 0]
        paired = paired_ref[0, slot, 0].astype(jnp.float32) * mask
        out_ref[slot, :, RANK:] = paired.astype(jnp.bfloat16)


def half_level(place, self_factors, partner_factors, link_mask):
    half = RANK // 2
    spec = pl.BlockSpec(
        (1, SLOTS, 1, half, RANK), lambda i, place: (place[0], 0, place[1], 0, 0)
    )
    shape = SLOTS, half, 2 * RANK
    split = LEVELS, SLOTS, 2, half, RANK
    return pl.pallas_call(
        level_kernel,
        out_shape=jax.ShapeDtypeStruct(shape, self_factors.dtype),
        grid_spec=pltpu.PrefetchScalarGridSpec(
            num_scalar_prefetch=1,
            grid=(1,),
            in_specs=[pl.BlockSpec(memory_space=pltpu.SMEM), spec, spec],
            out_specs=pl.BlockSpec(shape, lambda i, place: (0, 0, 0)),
        ),
        compiler_params=pltpu.CompilerParams(vmem_limit_bytes=60 * 2**20),
    )(place, link_mask, self_factors.reshape(split), partner_factors.reshape(split))


def body(panels, self_factors, partner_factors, link_mask, block_ranks):
    columns = panels.shape[1]
    zl_at = lax.axis_index("zl")
    odd = zl_at % 2
    place = jnp.stack([lax.axis_index("x"), odd]).astype(jnp.int32)

    own_half = exchange(half_level(place, self_factors, partner_factors, link_mask), PEERS)
    other_half = swap(own_half, "zl", 1)
    gram, panels = grams(panels)
    panels = once_done(panels, other_half, gram).reshape(SLOTS, RANK, columns)
    base = exchange(panels, PEERS)

    gram = gram + swap(gram, "x", 1)
    gram = gram + swap(gram, "x", 2)
    inverse = invert(zl_at.astype(jnp.int32).reshape(1), block_ranks, gram)
    halves = [jnp.where(odd == at, own_half, other_half) for at in range(2)]
    factors = by_place(along_x(jnp.concatenate(halves, axis=1), inverse))
    lower, upper = jnp.stack(factors[:2]), jnp.stack(factors[2:])

    level = near_levels(base, lower, columns)
    paired = swap(level, "core", 1)
    cross = sums_call(cross_kernel, (2, 4, 4, 32, RANK), upper, level, paired, base)

    cross = exchange(cross.reshape(2 * 4, 4, 32, RANK), ("yl", "x"))
    cross = cross.reshape(2, 4, 4, 2, 16, RANK).sum(1)
    cross = cross.transpose(1, 0, 2, 3, 4).reshape(16, 16, RANK)
    cross = exchange(cross, ("zh", "zl")).reshape(4, 4, 16, RANK).sum(1)
    pairs = jnp.stack([inverse, swap(inverse, "zl", 1)])
    pairs = [lax.dynamic_index_in_dim(pairs, zl_at % 2 ^ p, 0, False) for p in range(2)]
    inverse = jnp.concatenate(pairs, axis=0)
    solved = jnp.einsum("jrk,jkm->jrm", cross, inverse, precision=HIGHEST)
    return gather_halved(solved)


def solution(mesh):
    split = Mesh(mesh.devices.reshape(2, 2, 4, 2, 4, 4), ROW + COL)
    return jax.shard_map(
        body,
        mesh=split,
        in_specs=(P(ROW, COL), P(None, ROW, None), P(None, ROW, None), P(None, ROW), P(ROW)),
        out_specs=P(ROW, None),
        check_vma=False,
    )
```

```python
import math

import jax
import jax.numpy as jnp
from jax import lax
from jax.experimental import pallas as pl
from jax.experimental.pallas import tpu as pltpu
from jax.sharding import Mesh, PartitionSpec as P

RANK = 128
LEVELS = 4
SLOTS = 8
ROW = ("yh", "yl", "zh", "core")
COL = ("x", "zl")
PEERS = ("yl", "zh")
HIGHEST = lax.Precision.HIGHEST


def gram_kernel(panels_ref, out_ref, copy_ref):
    rows = lax.broadcasted_iota(jnp.int32, (RANK, RANK), 0)
    cols = lax.broadcasted_iota(jnp.int32, (RANK, RANK), 1)

    def gram(block):
        value = panels_ref[block * RANK : (block + 1) * RANK]
        return lax.dot_general(
            value, value, (((1,), (1,)), ((), ())), preferred_element_type=jnp.float32
        )

    for pair in range(out_ref.shape[0]):
        below, above = gram(2 * pair), gram(2 * pair + 1)
        out_ref[pair, :RANK] = jnp.where(rows >= cols, below, above)
        diagonal = jnp.sum(jnp.where(rows == cols, above, 0.0), axis=0, keepdims=True)
        out_ref[pair, RANK:] = jnp.broadcast_to(diagonal, (8, RANK))
    copy_ref[...] = panels_ref[:, panels_ref.shape[1] - copy_ref.shape[1] :]


def local_grams(panels, late):
    return pl.pallas_call(
        gram_kernel,
        out_shape=(
            jax.ShapeDtypeStruct((SLOTS // 2, RANK + 8, RANK), jnp.float32),
            jax.ShapeDtypeStruct((panels.shape[0], late), panels.dtype),
        ),
        in_specs=[pl.BlockSpec(memory_space=pltpu.VMEM)],
        out_specs=[pl.BlockSpec(memory_space=pltpu.VMEM)] * 2,
        compiler_params=pltpu.CompilerParams(vmem_limit_bytes=16 * 2**20),
    )(panels)


def invert_kernel(place_ref, ranks_ref, packed_ref, out_ref):
    lane = lax.broadcasted_iota(jnp.int32, (8, RANK), 1)
    sub = lax.broadcasted_iota(jnp.int32, (8, RANK), 0)
    rows = lax.broadcasted_iota(jnp.int32, (RANK, RANK), 0)
    cols = lax.broadcasted_iota(jnp.int32, (RANK, RANK), 1)
    blocks = out_ref.shape[0]
    packed = packed_ref[0, :RANK]
    turned = packed.T
    above = jnp.where(rows < cols, packed, turned)
    grams = (
        jnp.where(rows >= cols, packed, turned),
        jnp.where(rows == cols, packed_ref[0, RANK : RANK + 1], above),
    )
    ranks = [ranks_ref[place_ref[0] * blocks + b] for b in range(blocks)]
    tiles = []
    for b in range(blocks):
        kept = (rows < ranks[b]) & (cols < ranks[b])
        gram = jnp.where(kept, grams[b], jnp.where(rows == cols, 1.0, 0.0))
        tiles.append([gram[8 * g : 8 * g + 8] for g in range(RANK // 8)])
    for k in range(RANK):
        first, at = k // 8, k % 8
        for b in range(blocks):
            tile = tiles[b]
            row = tile[first][at : at + 1, :]
            scaled = jnp.where(lane[:1] == k, 1.0, row) / row[:, k : k + 1]
            for g in range(first, RANK // 8):
                column = tile[g][:, k : k + 1]
                clear = lane == k
                if g == first:
                    column = jnp.where(sub[:, :1] > at, column, 0.0)
                    clear = clear & (sub > at)
                tile[g] = jnp.where(clear, 0.0, tile[g]) - column * scaled
    for b in range(blocks):
        done = jnp.concatenate(tiles[b], axis=0)
        pivots = jnp.sum(jnp.where(rows == cols, done, 0.0), axis=1, keepdims=True)
        lower = jnp.where(rows > cols, done, jnp.where(rows == cols, 1.0, 0.0))
        inverse = lax.dot_general(
            lower,
            lower / pivots,
            (((0,), (0,)), ((), ())),
            precision=HIGHEST,
            preferred_element_type=jnp.float32,
        )
        out_ref[b] = jnp.where(rows < ranks[b], inverse * (4.0 * math.sqrt(RANK)), 0.0)


def invert(place, block_ranks, packed):
    smem = pl.BlockSpec(memory_space=pltpu.SMEM)
    return pl.pallas_call(
        invert_kernel,
        out_shape=jax.ShapeDtypeStruct((2, RANK, RANK), jnp.float32),
        in_specs=[smem, smem, pl.BlockSpec(memory_space=pltpu.VMEM)],
        out_specs=pl.BlockSpec(memory_space=pltpu.VMEM),
        compiler_params=pltpu.CompilerParams(vmem_limit_bytes=16 * 2**20),
    )(place, block_ranks, packed)


def factor_of(factors_ref, level, slot, flipped=False):
    factor = factors_ref[level % 2, slot]
    if flipped:
        factor = jnp.concatenate([factor[:, RANK:], factor[:, :RANK]], axis=1)
    return factor


def joint(factors_ref, level, slot, other):
    return jnp.concatenate(
        [
            factor_of(factors_ref, level, slot),
            factor_of(factors_ref, level, other, True),
        ],
        axis=0,
    )


def matmul(left, right):
    return jnp.dot(left, right, preferred_element_type=jnp.float32)


def near_levels_kernel(base_ref, factors_ref, *rest):
    out_ref, mid_ref = rest[-2:]
    columns = out_ref.shape[2]
    for source, target, level, bit in ((base_ref, mid_ref, 0, 1), (mid_ref, out_ref, 1, 4)):
        for slot in range(SLOTS):
            other = slot ^ bit
            if slot < other:
                rows = jnp.concatenate([source[slot, :, :columns], source[other, :, :columns]], axis=0)
                mixed = matmul(joint(factors_ref, level, slot, other), rows)
                mixed = mixed.astype(jnp.bfloat16)
                target[slot] = mixed[:RANK]
                target[other] = mixed[RANK:]


def near_levels(base, factors, columns, *after):
    vmem = pl.BlockSpec(memory_space=pltpu.VMEM)
    shape = SLOTS, RANK, columns
    return pl.pallas_call(
        near_levels_kernel,
        out_shape=jax.ShapeDtypeStruct(shape, base.dtype),
        in_specs=[vmem, vmem] + [pl.BlockSpec(memory_space=pl.ANY)] * len(after),
        out_specs=vmem,
        scratch_shapes=[pltpu.VMEM(shape, base.dtype)],
        compiler_params=pltpu.CompilerParams(vmem_limit_bytes=16 * 2**20),
    )(base, factors, *[corner(other) for other in after])


def sums_of(factors_ref, level_ref, paired_ref, base_ref, slot, other):
    def third(at):
        rows = jnp.concatenate([level_ref[at], paired_ref[at]], axis=0)
        return matmul(factor_of(factors_ref, 2, at), rows).astype(jnp.bfloat16)

    columns = level_ref.shape[2]
    rows = jnp.concatenate([third(slot), third(other)], axis=0)
    bases = jnp.concatenate([base_ref[slot, :, :columns], base_ref[other, :, :columns]], axis=0)
    return lax.dot_general(
        rows, bases, (((1,), (1,)), ((), ())), preferred_element_type=jnp.float32
    )


PAIRS = tuple((slot, slot ^ 2) for slot in range(SLOTS) if slot < slot ^ 2)


def early_kernel(factors_ref, level_ref, paired_ref, base_ref, out_ref):
    for at, (slot, other) in enumerate(PAIRS):
        out_ref[at] = sums_of(factors_ref, level_ref, paired_ref, base_ref, slot, other)


def cross_kernel(factors_ref, level_ref, paired_ref, base_ref, early_ref, out_ref):
    for at, (slot, other) in enumerate(PAIRS):
        sums = early_ref[at] + sums_of(
            factors_ref, level_ref, paired_ref, base_ref, slot, other
        )
        parts = []
        for _ in range(3):
            part = sums.astype(jnp.bfloat16)
            parts.append(part)
            sums = sums - part.astype(jnp.float32)
        factor = (
            factor_of(factors_ref, 3, slot),
            factor_of(factors_ref, 3, other, True),
        )
        for side, block in enumerate((slot, other)):
            side_of = slice(side * RANK, (side + 1) * RANK)
            cross = sum(matmul(factor[side], part[:, side_of]) for part in parts[::-1])
            for x in range(4):
                out_ref[block // 4, x, block % 4] = cross[32 * x : 32 * x + 32]


def sums_call(kernel, shape, *arrays):
    vmem = pl.BlockSpec(memory_space=pltpu.VMEM)
    return pl.pallas_call(
        kernel,
        out_shape=jax.ShapeDtypeStruct(shape, jnp.float32),
        in_specs=[vmem] * len(arrays),
        out_specs=vmem,
        compiler_params=pltpu.CompilerParams(vmem_limit_bytes=16 * 2**20),
    )(*arrays)


def nothing_kernel(*refs):
    del refs


def corner(value):
    value = value.reshape(-1, *value.shape[-2:])
    return value[0, :16, :RANK]


def once_done(value, *others):
    others = [corner(other) for other in others]
    return pl.pallas_call(
        nothing_kernel,
        out_shape=jax.ShapeDtypeStruct(value.shape, value.dtype),
        in_specs=[pl.BlockSpec(memory_space=pl.ANY)] * (1 + len(others)),
        out_specs=pl.BlockSpec(memory_space=pl.ANY),
        input_output_aliases={0: 0},
    )(value, *others)


def exchange(blocks, axes):
    return lax.all_to_all(blocks, axes, 0, 0, tiled=True)


def gather(block, axes):
    count = lax.axis_size(axes)
    return exchange(jnp.broadcast_to(block[None], (count,) + block.shape), axes)


def swap(block, axis, bit):
    return lax.ppermute(block, axis, [(i, i ^ bit) for i in range(lax.axis_size(axis))])


def along_x(block, *after):
    count = lax.axis_size("x")
    shift = lambda d: lax.ppermute(block, "x", [(i, (i - d) % count) for i in range(count)])
    own = once_done(block, *after) if after else block
    return jnp.stack([own] + [shift(d) for d in range(1, count)])


def part(blocks, at, count):
    return lax.dynamic_slice_in_dim(blocks, at * count, count, 0)


def grams(panels, late):
    zl_at = lax.axis_index("zl")
    packed, panels = local_grams(panels, late)
    total = part(packed, zl_at, 1)
    for other in range(1, 4):
        total = total + swap(part(packed, zl_at ^ other, 1), "zl", other)
    return total, panels


def by_place(every):
    x_at = lax.axis_index("x")
    return [lax.dynamic_index_in_dim(every, (x + 4 - x_at) % 4, 0, False) for x in range(4)]


def gather_halved(solved):
    blocks, rows, _ = solved.shape
    top = jnp.max(jnp.abs(solved), axis=2)
    power = jnp.clip(jnp.floor(jnp.log2(jnp.maximum(top, 1e-36))), -120.0, 120.0)
    values = (solved * jnp.exp2(-power)[:, :, None]).astype(jnp.float16)
    powers = jnp.pad(power.T.astype(jnp.float16), ((0, 0), (0, RANK - blocks)))
    sent = gather(jnp.concatenate([values, powers[None]], axis=0), COL)
    power = sent[:, blocks, :, :blocks].astype(jnp.float32).transpose(0, 2, 1)
    values = sent[:, :blocks].astype(jnp.float32) * jnp.exp2(power)[:, :, :, None]
    values = values.reshape(4, 2, 2, blocks, rows, RANK)
    return values.transpose(1, 3, 0, 2, 4, 5).reshape(-1, RANK)


def first_kernel(place_ref, mask_ref, panels_ref, own_ref, paired_ref, out_ref):
    columns = panels_ref.shape[1]
    half = RANK // 2
    for slot in range(SLOTS):
        mask = mask_ref[lax.shift_right_logical(place_ref[0], 1), slot].astype(jnp.float32)
        out_ref[slot, :, :columns] = panels_ref[slot * RANK : (slot + 1) * RANK]
        out_ref[slot, :half, columns:] = own_ref[0, slot, 0]
        paired = paired_ref[0, slot, 0].astype(jnp.float32) * mask
        out_ref[slot, half:, columns:] = paired.astype(jnp.bfloat16)


def first_part(place, panels, self_factors, partner_factors, link_mask, columns):
    half = RANK // 2
    spec = pl.BlockSpec(
        (1, SLOTS, 1, half, RANK),
        lambda i, place: (lax.shift_right_logical(place[0], 1), 0, place[0] & 1, 0, 0),
    )
    shape = SLOTS, RANK, columns + RANK
    split = LEVELS, SLOTS, 2, half, RANK
    return pl.pallas_call(
        first_kernel,
        out_shape=jax.ShapeDtypeStruct(shape, panels.dtype),
        grid_spec=pltpu.PrefetchScalarGridSpec(
            num_scalar_prefetch=1,
            grid=(1,),
            in_specs=[
                pl.BlockSpec(memory_space=pltpu.SMEM),
                pl.BlockSpec((panels.shape[0], columns), lambda i, place: (0, 0)),
                spec,
                spec,
            ],
            out_specs=pl.BlockSpec(shape, lambda i, place: (0, 0, 0)),
        ),
        compiler_params=pltpu.CompilerParams(vmem_limit_bytes=60 * 2**20),
    )(place, link_mask, panels, self_factors.reshape(split), partner_factors.reshape(split))


def body(panels, self_factors, partner_factors, link_mask, block_ranks):
    columns = panels.shape[1]
    early = columns // 8
    late = columns - early
    half = RANK // 2
    zl_at = lax.axis_index("zl")
    odd = zl_at % 2
    place = (lax.axis_index("x") * 2 + odd).astype(jnp.int32).reshape(1)

    first = first_part(place, panels, self_factors, partner_factors, link_mask, early)
    first = exchange(first, PEERS)
    own_half = first[:, :, early:]
    other_half = swap(own_half, "zl", 1)
    gram, panels = grams(panels, late)
    second = once_done(panels, other_half, gram).reshape(SLOTS, RANK, late)
    second = exchange(second, PEERS)

    gram = gram + swap(gram, "x", 1)
    gram = gram + swap(gram, "x", 2)
    inverse = invert(zl_at.astype(jnp.int32).reshape(1), block_ranks, gram)
    low, high = (jnp.where(odd == at, own_half, other_half) for at in range(2))
    factors = [jnp.concatenate([low[:, i], high[:, i]], axis=1) for i in (slice(half), slice(half, RANK))]
    factors = by_place(along_x(jnp.concatenate(factors, axis=2), inverse))
    lower, upper = jnp.stack(factors[:2]), jnp.stack(factors[2:])

    level = near_levels(first, lower, early)
    paired = swap(level, "core", 1)
    shape = len(PAIRS), 2 * RANK, 2 * RANK
    sums = sums_call(early_kernel, shape, upper, level, paired, first)
    level = near_levels(second, lower, late, sums)
    paired = swap(level, "core", 1)
    cross = sums_call(cross_kernel, (2, 4, 4, 32, RANK), upper, level, paired, second, sums)

    cross = exchange(cross.reshape(2 * 4, 4, 32, RANK), ("yl", "x"))
    cross = cross.reshape(2, 4, 4, 2, 16, RANK).sum(1)
    cross = cross.transpose(1, 0, 2, 3, 4).reshape(16, 16, RANK)
    cross = exchange(cross, ("zh", "zl")).reshape(4, 4, 16, RANK).sum(1)
    pairs = jnp.stack([inverse, swap(inverse, "zl", 1)])
    pairs = [lax.dynamic_index_in_dim(pairs, zl_at % 2 ^ p, 0, False) for p in range(2)]
    inverse = jnp.concatenate(pairs, axis=0)
    solved = jnp.einsum("jrk,jkm->jrm", cross, inverse, precision=HIGHEST)
    return gather_halved(solved)


def solution(mesh):
    split = Mesh(mesh.devices.reshape(2, 2, 4, 2, 4, 4), ROW + COL)
    return jax.shard_map(
        body,
        mesh=split,
        in_specs=(P(ROW, COL), P(None, ROW, None), P(None, ROW, None), P(None, ROW), P(ROW)),
        out_specs=P(ROW, None),
        check_vma=False,
    )
```

```python
import math

import jax
import jax.numpy as jnp
from jax import lax
from jax.experimental import pallas as pl
from jax.experimental.pallas import tpu as pltpu
from jax.sharding import Mesh, PartitionSpec as P

RANK = 128
LEVELS = 4
SLOTS = 8
ROW = ("yh", "yl", "zh", "core")
COL = ("x", "zl")
PEERS = ("yl", "zh")
HIGHEST = lax.Precision.HIGHEST


def gram_kernel(panels_ref, out_ref, copy_ref):
    rows = lax.broadcasted_iota(jnp.int32, (RANK, RANK), 0)
    cols = lax.broadcasted_iota(jnp.int32, (RANK, RANK), 1)

    def gram(block):
        value = panels_ref[block * RANK : (block + 1) * RANK]
        return lax.dot_general(
            value, value, (((1,), (1,)), ((), ())), preferred_element_type=jnp.float32
        )

    for pair in range(out_ref.shape[0]):
        below, above = gram(2 * pair), gram(2 * pair + 1)
        out_ref[pair, :RANK] = jnp.where(rows >= cols, below, above)
        diagonal = jnp.sum(jnp.where(rows == cols, above, 0.0), axis=0, keepdims=True)
        out_ref[pair, RANK:] = jnp.broadcast_to(diagonal, (8, RANK))
    copy_ref[...] = panels_ref[:, panels_ref.shape[1] - copy_ref.shape[1] :]


def local_grams(panels, late):
    return pl.pallas_call(
        gram_kernel,
        out_shape=(
            jax.ShapeDtypeStruct((SLOTS // 2, RANK + 8, RANK), jnp.float32),
            jax.ShapeDtypeStruct((panels.shape[0], late), panels.dtype),
        ),
        in_specs=[pl.BlockSpec(memory_space=pltpu.VMEM)],
        out_specs=[pl.BlockSpec(memory_space=pltpu.VMEM)] * 2,
        compiler_params=pltpu.CompilerParams(vmem_limit_bytes=16 * 2**20),
    )(panels)


def invert_kernel(place_ref, ranks_ref, packed_ref, out_ref):
    lane = lax.broadcasted_iota(jnp.int32, (8, RANK), 1)
    sub = lax.broadcasted_iota(jnp.int32, (8, RANK), 0)
    rows = lax.broadcasted_iota(jnp.int32, (RANK, RANK), 0)
    cols = lax.broadcasted_iota(jnp.int32, (RANK, RANK), 1)
    blocks = out_ref.shape[0]
    packed = packed_ref[0, :RANK]
    turned = packed.T
    above = jnp.where(rows < cols, packed, turned)
    grams = (
        jnp.where(rows >= cols, packed, turned),
        jnp.where(rows == cols, packed_ref[0, RANK : RANK + 1], above),
    )
    ranks = [ranks_ref[place_ref[0] * blocks + b] for b in range(blocks)]
    tiles = []
    for b in range(blocks):
        kept = (rows < ranks[b]) & (cols < ranks[b])
        gram = jnp.where(kept, grams[b], jnp.where(rows == cols, 1.0, 0.0))
        tiles.append([gram[8 * g : 8 * g + 8] for g in range(RANK // 8)])
    for k in range(RANK):
        first, at = k // 8, k % 8
        for b in range(blocks):
            tile = tiles[b]
            row = tile[first][at : at + 1, :]
            scaled = jnp.where(lane[:1] == k, 1.0, row) / row[:, k : k + 1]
            for g in range(first, RANK // 8):
                column = tile[g][:, k : k + 1]
                clear = lane == k
                if g == first:
                    column = jnp.where(sub[:, :1] > at, column, 0.0)
                    clear = clear & (sub > at)
                tile[g] = jnp.where(clear, 0.0, tile[g]) - column * scaled
    for b in range(blocks):
        done = jnp.concatenate(tiles[b], axis=0)
        pivots = jnp.sum(jnp.where(rows == cols, done, 0.0), axis=1, keepdims=True)
        lower = jnp.where(rows > cols, done, jnp.where(rows == cols, 1.0, 0.0))
        inverse = lax.dot_general(
            lower,
            lower / pivots,
            (((0,), (0,)), ((), ())),
            precision=HIGHEST,
            preferred_element_type=jnp.float32,
        )
        out_ref[b] = jnp.where(rows < ranks[b], inverse * (4.0 * math.sqrt(RANK)), 0.0)


def invert(place, block_ranks, packed):
    smem = pl.BlockSpec(memory_space=pltpu.SMEM)
    return pl.pallas_call(
        invert_kernel,
        out_shape=jax.ShapeDtypeStruct((2, RANK, RANK), jnp.float32),
        in_specs=[smem, smem, pl.BlockSpec(memory_space=pltpu.VMEM)],
        out_specs=pl.BlockSpec(memory_space=pltpu.VMEM),
        compiler_params=pltpu.CompilerParams(vmem_limit_bytes=16 * 2**20),
    )(place, block_ranks, packed)


def factor_of(factors_ref, level, slot, flipped=False):
    factor = factors_ref[level % 2, slot]
    if flipped:
        factor = jnp.concatenate([factor[:, RANK:], factor[:, :RANK]], axis=1)
    return factor


def joint(factors_ref, level, slot, other):
    return jnp.concatenate(
        [
            factor_of(factors_ref, level, slot),
            factor_of(factors_ref, level, other, True),
        ],
        axis=0,
    )


def matmul(left, right):
    return jnp.dot(left, right, preferred_element_type=jnp.float32)


def near_levels_kernel(base_ref, factors_ref, *rest):
    out_ref, mid_ref = rest[-2:]
    columns = out_ref.shape[2]
    for source, target, level, bit in ((base_ref, mid_ref, 0, 1), (mid_ref, out_ref, 1, 4)):
        for slot in range(SLOTS):
            other = slot ^ bit
            if slot < other:
                rows = jnp.concatenate([source[slot, :, :columns], source[other, :, :columns]], axis=0)
                mixed = matmul(joint(factors_ref, level, slot, other), rows)
                mixed = mixed.astype(jnp.bfloat16)
                target[slot] = mixed[:RANK]
                target[other] = mixed[RANK:]


def near_levels(base, factors, columns, *after):
    vmem = pl.BlockSpec(memory_space=pltpu.VMEM)
    shape = SLOTS, RANK, columns
    return pl.pallas_call(
        near_levels_kernel,
        out_shape=jax.ShapeDtypeStruct(shape, base.dtype),
        in_specs=[vmem, vmem] + [pl.BlockSpec(memory_space=pl.ANY)] * len(after),
        out_specs=vmem,
        scratch_shapes=[pltpu.VMEM(shape, base.dtype)],
        compiler_params=pltpu.CompilerParams(vmem_limit_bytes=16 * 2**20),
    )(base, factors, *[corner(other) for other in after])


def sums_of(factors_ref, level_ref, paired_ref, base_ref, slot, other):
    def third(at):
        rows = jnp.concatenate([level_ref[at], paired_ref[at]], axis=0)
        return matmul(factor_of(factors_ref, 2, at), rows).astype(jnp.bfloat16)

    columns = level_ref.shape[2]
    rows = jnp.concatenate([third(slot), third(other)], axis=0)
    bases = jnp.concatenate([base_ref[slot, :, :columns], base_ref[other, :, :columns]], axis=0)
    return lax.dot_general(
        rows, bases, (((1,), (1,)), ((), ())), preferred_element_type=jnp.float32
    )


PAIRS = tuple((slot, slot ^ 2) for slot in range(SLOTS) if slot < slot ^ 2)


def early_kernel(factors_ref, level_ref, paired_ref, base_ref, out_ref):
    for at, (slot, other) in enumerate(PAIRS):
        out_ref[at] = sums_of(factors_ref, level_ref, paired_ref, base_ref, slot, other)


def cross_kernel(factors_ref, level_ref, paired_ref, base_ref, early_ref, out_ref):
    for at, (slot, other) in enumerate(PAIRS):
        sums = early_ref[at] + sums_of(
            factors_ref, level_ref, paired_ref, base_ref, slot, other
        )
        parts = []
        for _ in range(3):
            part = sums.astype(jnp.bfloat16)
            parts.append(part)
            sums = sums - part.astype(jnp.float32)
        factor = (
            factor_of(factors_ref, 3, slot),
            factor_of(factors_ref, 3, other, True),
        )
        for side, block in enumerate((slot, other)):
            side_of = slice(side * RANK, (side + 1) * RANK)
            cross = matmul(factor[side], jnp.concatenate([part[:, side_of] for part in parts], axis=1))
            cross = cross[:, 2 * RANK :] + cross[:, RANK : 2 * RANK] + cross[:, :RANK]
            for x in range(4):
                out_ref[block // 4, x, block % 4] = cross[32 * x : 32 * x + 32]


def sums_call(kernel, shape, *arrays):
    vmem = pl.BlockSpec(memory_space=pltpu.VMEM)
    return pl.pallas_call(
        kernel,
        out_shape=jax.ShapeDtypeStruct(shape, jnp.float32),
        in_specs=[vmem] * len(arrays),
        out_specs=vmem,
        compiler_params=pltpu.CompilerParams(vmem_limit_bytes=16 * 2**20),
    )(*arrays)


def nothing_kernel(*refs):
    del refs


def corner(value):
    value = value.reshape(-1, *value.shape[-2:])
    return value[0, :16, :RANK]


def once_done(value, *others):
    others = [corner(other) for other in others]
    return pl.pallas_call(
        nothing_kernel,
        out_shape=jax.ShapeDtypeStruct(value.shape, value.dtype),
        in_specs=[pl.BlockSpec(memory_space=pl.ANY)] * (1 + len(others)),
        out_specs=pl.BlockSpec(memory_space=pl.ANY),
        input_output_aliases={0: 0},
    )(value, *others)


def exchange(blocks, axes):
    return lax.all_to_all(blocks, axes, 0, 0, tiled=True)


def gather(block, axes):
    count = lax.axis_size(axes)
    return exchange(jnp.broadcast_to(block[None], (count,) + block.shape), axes)


def swap(block, axis, bit):
    return lax.ppermute(block, axis, [(i, i ^ bit) for i in range(lax.axis_size(axis))])


def along_x(block, *after):
    count = lax.axis_size("x")
    shift = lambda d: lax.ppermute(block, "x", [(i, (i - d) % count) for i in range(count)])
    own = once_done(block, *after) if after else block
    return jnp.stack([own] + [shift(d) for d in range(1, count)])


def part(blocks, at, count):
    return lax.dynamic_slice_in_dim(blocks, at * count, count, 0)


def grams(panels, late):
    zl_at = lax.axis_index("zl")
    packed, panels = local_grams(panels, late)
    total = part(packed, zl_at, 1)
    for other in range(1, 4):
        total = total + swap(part(packed, zl_at ^ other, 1), "zl", other)
    return total, panels


def by_place(every):
    x_at = lax.axis_index("x")
    return [lax.dynamic_index_in_dim(every, (x + 4 - x_at) % 4, 0, False) for x in range(4)]


def gather_halved(solved):
    blocks, rows, _ = solved.shape
    top = jnp.max(jnp.abs(solved), axis=2)
    power = jnp.clip(jnp.floor(jnp.log2(jnp.maximum(top, 1e-36))), -120.0, 120.0)
    values = (solved * jnp.exp2(-power)[:, :, None]).astype(jnp.float16).reshape(-1, 8, RANK)
    powers = power.astype(jnp.float16).reshape(1, 1, blocks * rows)
    powers = jnp.pad(powers, ((0, 0), (0, 7), (0, RANK - blocks * rows)))
    sent = gather(jnp.concatenate([values, powers], axis=0), COL)
    power = sent[:, -1, 0, : blocks * rows].astype(jnp.float32).reshape(-1, blocks, rows)
    values = sent[:, :-1].astype(jnp.float32).reshape(-1, blocks, rows, RANK)
    values = values * jnp.exp2(power)[:, :, :, None]
    values = values.reshape(4, 2, 2, blocks, rows, RANK)
    return values.transpose(1, 3, 0, 2, 4, 5).reshape(-1, RANK)


def first_kernel(place_ref, mask_ref, panels_ref, own_ref, paired_ref, out_ref):
    columns = panels_ref.shape[1]
    half = RANK // 2
    for slot in range(SLOTS):
        mask = mask_ref[lax.shift_right_logical(place_ref[0], 1), slot].astype(jnp.float32)
        out_ref[slot, :, :columns] = panels_ref[slot * RANK : (slot + 1) * RANK]
        out_ref[slot, :half, columns:] = own_ref[0, slot, 0]
        paired = paired_ref[0, slot, 0].astype(jnp.float32) * mask
        out_ref[slot, half:, columns:] = paired.astype(jnp.bfloat16)


def first_part(place, panels, self_factors, partner_factors, link_mask, columns):
    half = RANK // 2
    spec = pl.BlockSpec(
        (1, SLOTS, 1, half, RANK),
        lambda i, place: (lax.shift_right_logical(place[0], 1), 0, place[0] & 1, 0, 0),
    )
    shape = SLOTS, RANK, columns + RANK
    split = LEVELS, SLOTS, 2, half, RANK
    return pl.pallas_call(
        first_kernel,
        out_shape=jax.ShapeDtypeStruct(shape, panels.dtype),
        grid_spec=pltpu.PrefetchScalarGridSpec(
            num_scalar_prefetch=1,
            grid=(1,),
            in_specs=[
                pl.BlockSpec(memory_space=pltpu.SMEM),
                pl.BlockSpec((panels.shape[0], columns), lambda i, place: (0, 0)),
                spec,
                spec,
            ],
            out_specs=pl.BlockSpec(shape, lambda i, place: (0, 0, 0)),
        ),
        compiler_params=pltpu.CompilerParams(vmem_limit_bytes=60 * 2**20),
    )(place, link_mask, panels, self_factors.reshape(split), partner_factors.reshape(split))


def body(panels, self_factors, partner_factors, link_mask, block_ranks):
    columns = panels.shape[1]
    early = columns // 8
    late = columns - early
    half = RANK // 2
    zl_at = lax.axis_index("zl")
    odd = zl_at % 2
    place = (lax.axis_index("x") * 2 + odd).astype(jnp.int32).reshape(1)

    first = first_part(place, panels, self_factors, partner_factors, link_mask, early)
    first = exchange(first, PEERS)
    own_half = first[:, :, early:]
    other_half = swap(own_half, "zl", 1)
    gram, panels = grams(panels, late)
    second = once_done(panels, other_half, gram).reshape(SLOTS, RANK, late)
    second = exchange(second, PEERS)

    gram = gram + swap(gram, "x", 1)
    gram = gram + swap(gram, "x", 2)
    inverse = invert(zl_at.astype(jnp.int32).reshape(1), block_ranks, gram)
    low, high = (jnp.where(odd == at, own_half, other_half) for at in range(2))
    factors = [jnp.concatenate([low[:, i], high[:, i]], axis=1) for i in (slice(half), slice(half, RANK))]
    factors = by_place(along_x(jnp.concatenate(factors, axis=2), inverse))
    lower, upper = jnp.stack(factors[:2]), jnp.stack(factors[2:])

    level = near_levels(first, lower, early)
    paired = swap(level, "core", 1)
    shape = len(PAIRS), 2 * RANK, 2 * RANK
    sums = sums_call(early_kernel, shape, upper, level, paired, first)
    level = near_levels(second, lower, late, sums)
    paired = swap(level, "core", 1)
    cross = sums_call(cross_kernel, (2, 4, 4, 32, RANK), upper, level, paired, second, sums)

    cross = exchange(cross.reshape(2 * 4, 4, 32, RANK), ("yl", "x"))
    cross = cross.reshape(2, 4, 4, 2, 16, RANK).sum(1)
    cross = cross.transpose(1, 0, 2, 3, 4).reshape(16, 16, RANK)
    cross = exchange(cross, ("zh", "zl")).reshape(4, 4, 16, RANK).sum(1)
    pairs = jnp.stack([inverse, swap(inverse, "zl", 1)])
    pairs = [lax.dynamic_index_in_dim(pairs, zl_at % 2 ^ p, 0, False) for p in range(2)]
    inverse = jnp.concatenate(pairs, axis=0)
    solved = jnp.einsum("jrk,jkm->jrm", cross, inverse, precision=HIGHEST)
    return gather_halved(solved)


def solution(mesh):
    split = Mesh(mesh.devices.reshape(2, 2, 4, 2, 4, 4), ROW + COL)
    return jax.shard_map(
        body,
        mesh=split,
        in_specs=(P(ROW, COL), P(None, ROW, None), P(None, ROW, None), P(None, ROW), P(ROW)),
        out_specs=P(ROW, None),
        check_vma=False,
    )
```

```python
import math

import jax
import jax.numpy as jnp
from jax import lax
from jax.experimental import pallas as pl
from jax.experimental.pallas import tpu as pltpu
from jax.sharding import Mesh, PartitionSpec as P

RANK = 128
LEVELS = 4
SLOTS = 8
ROW = ("yh", "yl", "zh", "core")
COL = ("x", "zl")
PEERS = ("yl", "zh")
HIGHEST = lax.Precision.HIGHEST


def gram_kernel(panels_ref, out_ref, copy_ref):
    rows = lax.broadcasted_iota(jnp.int32, (RANK, RANK), 0)
    cols = lax.broadcasted_iota(jnp.int32, (RANK, RANK), 1)

    def gram(block):
        value = panels_ref[block * RANK : (block + 1) * RANK]
        return lax.dot_general(
            value, value, (((1,), (1,)), ((), ())), preferred_element_type=jnp.float32
        )

    for pair in range(out_ref.shape[0]):
        below, above = gram(2 * pair), gram(2 * pair + 1)
        out_ref[pair, :RANK] = jnp.where(rows >= cols, below, above)
        diagonal = jnp.sum(jnp.where(rows == cols, above, 0.0), axis=0, keepdims=True)
        out_ref[pair, RANK:] = jnp.broadcast_to(diagonal, (8, RANK))
    copy_ref[...] = panels_ref[:, panels_ref.shape[1] - copy_ref.shape[1] :]


def local_grams(panels, late):
    return pl.pallas_call(
        gram_kernel,
        out_shape=(
            jax.ShapeDtypeStruct((SLOTS // 2, RANK + 8, RANK), jnp.float32),
            jax.ShapeDtypeStruct((panels.shape[0], late), panels.dtype),
        ),
        in_specs=[pl.BlockSpec(memory_space=pltpu.VMEM)],
        out_specs=[pl.BlockSpec(memory_space=pltpu.VMEM)] * 2,
        compiler_params=pltpu.CompilerParams(vmem_limit_bytes=16 * 2**20),
    )(panels)


def invert_kernel(place_ref, ranks_ref, packed_ref, out_ref):
    lane = lax.broadcasted_iota(jnp.int32, (8, RANK), 1)
    sub = lax.broadcasted_iota(jnp.int32, (8, RANK), 0)
    rows = lax.broadcasted_iota(jnp.int32, (RANK, RANK), 0)
    cols = lax.broadcasted_iota(jnp.int32, (RANK, RANK), 1)
    blocks = out_ref.shape[0]
    packed = packed_ref[0, :RANK]
    turned = packed.T
    above = jnp.where(rows < cols, packed, turned)
    grams = (
        jnp.where(rows >= cols, packed, turned),
        jnp.where(rows == cols, packed_ref[0, RANK : RANK + 1], above),
    )
    ranks = [ranks_ref[place_ref[0] * blocks + b] for b in range(blocks)]
    tiles = []
    for b in range(blocks):
        kept = (rows < ranks[b]) & (cols < ranks[b])
        gram = jnp.where(kept, grams[b], jnp.where(rows == cols, 1.0, 0.0))
        tiles.append([gram[8 * g : 8 * g + 8] for g in range(RANK // 8)])
    for k in range(RANK):
        first, at = k // 8, k % 8
        for b in range(blocks):
            tile = tiles[b]
            row = tile[first][at : at + 1, :]
            scaled = jnp.where(lane[:1] == k, 1.0, row) / row[:, k : k + 1]
            for g in range(first, RANK // 8):
                column = tile[g][:, k : k + 1]
                clear = lane == k
                if g == first:
                    column = jnp.where(sub[:, :1] > at, column, 0.0)
                    clear = clear & (sub > at)
                tile[g] = jnp.where(clear, 0.0, tile[g]) - column * scaled
    for b in range(blocks):
        done = jnp.concatenate(tiles[b], axis=0)
        pivots = jnp.sum(jnp.where(rows == cols, done, 0.0), axis=1, keepdims=True)
        lower = jnp.where(rows > cols, done, jnp.where(rows == cols, 1.0, 0.0))
        inverse = lax.dot_general(
            lower,
            lower / pivots,
            (((0,), (0,)), ((), ())),
            precision=HIGHEST,
            preferred_element_type=jnp.float32,
        )
        out_ref[b] = jnp.where(rows < ranks[b], inverse * (4.0 * math.sqrt(RANK)), 0.0)


def invert(place, block_ranks, packed):
    smem = pl.BlockSpec(memory_space=pltpu.SMEM)
    return pl.pallas_call(
        invert_kernel,
        out_shape=jax.ShapeDtypeStruct((2, RANK, RANK), jnp.float32),
        in_specs=[smem, smem, pl.BlockSpec(memory_space=pltpu.VMEM)],
        out_specs=pl.BlockSpec(memory_space=pltpu.VMEM),
        compiler_params=pltpu.CompilerParams(vmem_limit_bytes=16 * 2**20),
    )(place, block_ranks, packed)


def factor_of(factors_ref, level, slot, flipped=False):
    factor = factors_ref[level % 2, slot]
    if flipped:
        factor = jnp.concatenate([factor[:, RANK:], factor[:, :RANK]], axis=1)
    return factor


def joint(factors_ref, level, slot, other):
    return jnp.concatenate(
        [
            factor_of(factors_ref, level, slot),
            factor_of(factors_ref, level, other, True),
        ],
        axis=0,
    )


def matmul(left, right):
    return jnp.dot(left, right, preferred_element_type=jnp.float32)


def near_levels_kernel(base_ref, factors_ref, *rest):
    out_ref, mid_ref = rest[-2:]
    columns = out_ref.shape[2]
    for source, target, level, bit in ((base_ref, mid_ref, 0, 1), (mid_ref, out_ref, 1, 4)):
        for slot in range(SLOTS):
            other = slot ^ bit
            if slot < other:
                rows = jnp.concatenate([source[slot, :, :columns], source[other, :, :columns]], axis=0)
                mixed = matmul(joint(factors_ref, level, slot, other), rows)
                mixed = mixed.astype(jnp.bfloat16)
                target[slot] = mixed[:RANK]
                target[other] = mixed[RANK:]


def near_levels(base, factors, columns, *after):
    vmem = pl.BlockSpec(memory_space=pltpu.VMEM)
    shape = SLOTS, RANK, columns
    return pl.pallas_call(
        near_levels_kernel,
        out_shape=jax.ShapeDtypeStruct(shape, base.dtype),
        in_specs=[vmem, vmem] + [pl.BlockSpec(memory_space=pl.ANY)] * len(after),
        out_specs=vmem,
        scratch_shapes=[pltpu.VMEM(shape, base.dtype)],
        compiler_params=pltpu.CompilerParams(vmem_limit_bytes=16 * 2**20),
    )(base, factors, *[corner(other) for other in after])


def sums_of(factors_ref, level_ref, paired_ref, base_ref, slot, other):
    def third(at):
        rows = jnp.concatenate([level_ref[at], paired_ref[at]], axis=0)
        return matmul(factor_of(factors_ref, 2, at), rows).astype(jnp.bfloat16)

    columns = level_ref.shape[2]
    rows = jnp.concatenate([third(slot), third(other)], axis=0)
    bases = jnp.concatenate([base_ref[slot, :, :columns], base_ref[other, :, :columns]], axis=0)
    return lax.dot_general(
        rows, bases, (((1,), (1,)), ((), ())), preferred_element_type=jnp.float32
    )


PAIRS = tuple((slot, slot ^ 2) for slot in range(SLOTS) if slot < slot ^ 2)


def early_kernel(factors_ref, level_ref, paired_ref, base_ref, out_ref):
    for at, (slot, other) in enumerate(PAIRS):
        out_ref[at] = sums_of(factors_ref, level_ref, paired_ref, base_ref, slot, other)


def cross_kernel(factors_ref, level_ref, paired_ref, base_ref, early_ref, out_ref):
    for at, (slot, other) in enumerate(PAIRS):
        sums = early_ref[at] + sums_of(
            factors_ref, level_ref, paired_ref, base_ref, slot, other
        )
        parts = []
        for _ in range(3):
            part = sums.astype(jnp.bfloat16)
            parts.append(part)
            sums = sums - part.astype(jnp.float32)
        factor = (
            factor_of(factors_ref, 3, slot),
            factor_of(factors_ref, 3, other, True),
        )
        for side, block in enumerate((slot, other)):
            side_of = slice(side * RANK, (side + 1) * RANK)
            cross = matmul(factor[side], jnp.concatenate([part[:, side_of] for part in parts], axis=1))
            cross = cross[:, 2 * RANK :] + cross[:, RANK : 2 * RANK] + cross[:, :RANK]
            for x in range(4):
                out_ref[block // 4, x, block % 4] = cross[32 * x : 32 * x + 32]


def sums_call(kernel, shape, *arrays):
    vmem = pl.BlockSpec(memory_space=pltpu.VMEM)
    return pl.pallas_call(
        kernel,
        out_shape=jax.ShapeDtypeStruct(shape, jnp.float32),
        in_specs=[vmem] * len(arrays),
        out_specs=vmem,
        compiler_params=pltpu.CompilerParams(vmem_limit_bytes=16 * 2**20),
    )(*arrays)


def nothing_kernel(*refs):
    del refs


def corner(value):
    value = value.reshape(-1, *value.shape[-2:])
    return value[0, :16, :RANK]


def once_done(value, *others):
    others = [corner(other) for other in others]
    return pl.pallas_call(
        nothing_kernel,
        out_shape=jax.ShapeDtypeStruct(value.shape, value.dtype),
        in_specs=[pl.BlockSpec(memory_space=pl.ANY)] * (1 + len(others)),
        out_specs=pl.BlockSpec(memory_space=pl.ANY),
        input_output_aliases={0: 0},
    )(value, *others)


def exchange(blocks, axes):
    return lax.all_to_all(blocks, axes, 0, 0, tiled=True)


def gather(block, axes):
    count = lax.axis_size(axes)
    return exchange(jnp.broadcast_to(block[None], (count,) + block.shape), axes)


def swap(block, axis, bit):
    return lax.ppermute(block, axis, [(i, i ^ bit) for i in range(lax.axis_size(axis))])


def along_x(block, *after):
    count = lax.axis_size("x")
    shift = lambda d: lax.ppermute(block, "x", [(i, (i - d) % count) for i in range(count)])
    own = once_done(block, *after) if after else block
    return jnp.stack([own] + [shift(d) for d in range(1, count)])


def part(blocks, at, count):
    return lax.dynamic_slice_in_dim(blocks, at * count, count, 0)


def grams(panels, late):
    zl_at = lax.axis_index("zl")
    packed, panels = local_grams(panels, late)
    total = part(packed, zl_at, 1)
    for other in range(1, 4):
        total = total + swap(part(packed, zl_at ^ other, 1), "zl", other)
    return total, panels


def by_place(every):
    x_at = lax.axis_index("x")
    return [lax.dynamic_index_in_dim(every, (x + 4 - x_at) % 4, 0, False) for x in range(4)]


def gather_halved(solved):
    blocks, rows, _ = solved.shape
    top = jnp.max(jnp.abs(solved), axis=2)
    power = jnp.clip(jnp.floor(jnp.log2(jnp.maximum(top, 1e-36))), -120.0, 120.0)
    values = (solved * jnp.exp2(-power)[:, :, None]).astype(jnp.float16).reshape(-1, 8, RANK)
    powers = power.astype(jnp.float16).reshape(1, 1, blocks * rows)
    powers = jnp.pad(powers, ((0, 0), (0, 7), (0, RANK - blocks * rows)))
    sent = gather(jnp.concatenate([values, powers], axis=0), COL)
    power = sent[:, -1, 0, : blocks * rows].astype(jnp.float32).reshape(-1, blocks, rows)
    values = sent[:, :-1].astype(jnp.float32).reshape(-1, blocks, rows, RANK)
    values = values * jnp.exp2(power)[:, :, :, None]
    values = values.reshape(4, 2, 2, blocks, rows, RANK)
    return values.transpose(1, 3, 0, 2, 4, 5).reshape(-1, RANK)


def first_kernel(place_ref, mask_ref, panels_ref, own_ref, paired_ref, out_ref):
    columns = panels_ref.shape[1]
    half = RANK // 2
    for slot in range(SLOTS):
        mask = mask_ref[lax.shift_right_logical(place_ref[0], 1), slot].astype(jnp.float32)
        out_ref[slot, :, :columns] = panels_ref[slot * RANK : (slot + 1) * RANK]
        out_ref[slot, :half, columns:] = own_ref[0, slot, 0]
        paired = paired_ref[0, slot, 0].astype(jnp.float32) * mask
        out_ref[slot, half:, columns:] = paired.astype(jnp.bfloat16)


def first_part(place, panels, self_factors, partner_factors, link_mask, columns):
    half = RANK // 2
    spec = pl.BlockSpec(
        (1, SLOTS, 1, half, RANK),
        lambda i, place: (lax.shift_right_logical(place[0], 1), 0, place[0] & 1, 0, 0),
    )
    shape = SLOTS, RANK, columns + RANK
    split = LEVELS, SLOTS, 2, half, RANK
    return pl.pallas_call(
        first_kernel,
        out_shape=jax.ShapeDtypeStruct(shape, panels.dtype),
        grid_spec=pltpu.PrefetchScalarGridSpec(
            num_scalar_prefetch=1,
            grid=(1,),
            in_specs=[
                pl.BlockSpec(memory_space=pltpu.SMEM),
                pl.BlockSpec((panels.shape[0], columns), lambda i, place: (0, 0)),
                spec,
                spec,
            ],
            out_specs=pl.BlockSpec(shape, lambda i, place: (0, 0, 0)),
        ),
        compiler_params=pltpu.CompilerParams(vmem_limit_bytes=60 * 2**20),
    )(place, link_mask, panels, self_factors.reshape(split), partner_factors.reshape(split))


def body(panels, self_factors, partner_factors, link_mask, block_ranks):
    columns = panels.shape[1]
    early = columns // 4
    late = columns - early
    half = RANK // 2
    zl_at = lax.axis_index("zl")
    odd = zl_at % 2
    place = (lax.axis_index("x") * 2 + odd).astype(jnp.int32).reshape(1)

    first = first_part(place, panels, self_factors, partner_factors, link_mask, early)
    first = exchange(first, PEERS)
    own_half = first[:, :, early:]
    other_half = swap(own_half, "zl", 1)
    gram, panels = grams(panels, late)
    second = once_done(panels, other_half, gram).reshape(SLOTS, RANK, late)
    second = exchange(second, PEERS)

    gram = gram + swap(gram, "x", 1)
    gram = gram + swap(gram, "x", 2)
    inverse = invert(zl_at.astype(jnp.int32).reshape(1), block_ranks, gram)
    low, high = (jnp.where(odd == at, own_half, other_half) for at in range(2))
    factors = [jnp.concatenate([low[:, i], high[:, i]], axis=1) for i in (slice(half), slice(half, RANK))]
    factors = by_place(along_x(jnp.concatenate(factors, axis=2), inverse))
    lower, upper = jnp.stack(factors[:2]), jnp.stack(factors[2:])

    level = near_levels(first, lower, early)
    paired = swap(level, "core", 1)
    shape = len(PAIRS), 2 * RANK, 2 * RANK
    sums = sums_call(early_kernel, shape, upper, level, paired, first)
    level = near_levels(second, lower, late, sums)
    paired = swap(level, "core", 1)
    cross = sums_call(cross_kernel, (2, 4, 4, 32, RANK), upper, level, paired, second, sums)

    cross = exchange(cross.reshape(2 * 4, 4, 32, RANK), ("yl", "x"))
    cross = cross.reshape(2, 4, 4, 2, 16, RANK).sum(1)
    cross = cross.transpose(1, 0, 2, 3, 4).reshape(16, 16, RANK)
    cross = exchange(cross, ("zh", "zl")).reshape(4, 4, 16, RANK).sum(1)
    pairs = jnp.stack([inverse, swap(inverse, "zl", 1)])
    pairs = [lax.dynamic_index_in_dim(pairs, zl_at % 2 ^ p, 0, False) for p in range(2)]
    inverse = jnp.concatenate(pairs, axis=0)
    solved = jnp.einsum("jrk,jkm->jrm", cross, inverse, precision=HIGHEST)
    return gather_halved(solved)


def solution(mesh):
    split = Mesh(mesh.devices.reshape(2, 2, 4, 2, 4, 4), ROW + COL)
    return jax.shard_map(
        body,
        mesh=split,
        in_specs=(P(ROW, COL), P(None, ROW, None), P(None, ROW, None), P(None, ROW), P(ROW)),
        out_specs=P(ROW, None),
        check_vma=False,
    )
```

```python
import math

import jax
import jax.numpy as jnp
from jax import lax
from jax.experimental import pallas as pl
from jax.experimental.pallas import tpu as pltpu
from jax.sharding import Mesh, PartitionSpec as P

RANK = 128
LEVELS = 4
SLOTS = 8
ROW = ("yh", "yl", "zh", "core")
COL = ("x", "zl")
PEERS = ("yl", "zh")
HIGHEST = lax.Precision.HIGHEST


def gram_kernel(panels_ref, out_ref, copy_ref):
    rows = lax.broadcasted_iota(jnp.int32, (RANK, RANK), 0)
    cols = lax.broadcasted_iota(jnp.int32, (RANK, RANK), 1)

    def gram(block):
        value = panels_ref[block * RANK : (block + 1) * RANK]
        return lax.dot_general(
            value, value, (((1,), (1,)), ((), ())), preferred_element_type=jnp.float32
        )

    for pair in range(out_ref.shape[0]):
        below, above = gram(2 * pair), gram(2 * pair + 1)
        out_ref[pair, :RANK] = jnp.where(rows >= cols, below, above)
        diagonal = jnp.sum(jnp.where(rows == cols, above, 0.0), axis=0, keepdims=True)
        out_ref[pair, RANK:] = jnp.broadcast_to(diagonal, (8, RANK))
    copy_ref[...] = panels_ref[:, panels_ref.shape[1] - copy_ref.shape[1] :]


def local_grams(panels, late):
    return pl.pallas_call(
        gram_kernel,
        out_shape=(
            jax.ShapeDtypeStruct((SLOTS // 2, RANK + 8, RANK), jnp.float32),
            jax.ShapeDtypeStruct((panels.shape[0], late), panels.dtype),
        ),
        in_specs=[pl.BlockSpec(memory_space=pltpu.VMEM)],
        out_specs=[pl.BlockSpec(memory_space=pltpu.VMEM)] * 2,
        compiler_params=pltpu.CompilerParams(vmem_limit_bytes=16 * 2**20),
    )(panels)


def invert_kernel(place_ref, ranks_ref, packed_ref, out_ref):
    lane = lax.broadcasted_iota(jnp.int32, (8, RANK), 1)
    sub = lax.broadcasted_iota(jnp.int32, (8, RANK), 0)
    rows = lax.broadcasted_iota(jnp.int32, (RANK, RANK), 0)
    cols = lax.broadcasted_iota(jnp.int32, (RANK, RANK), 1)
    blocks = out_ref.shape[0]
    packed = packed_ref[0, :RANK]
    turned = packed.T
    above = jnp.where(rows < cols, packed, turned)
    grams = (
        jnp.where(rows >= cols, packed, turned),
        jnp.where(rows == cols, packed_ref[0, RANK : RANK + 1], above),
    )
    ranks = [ranks_ref[place_ref[0] * blocks + b] for b in range(blocks)]
    tiles = []
    for b in range(blocks):
        kept = (rows < ranks[b]) & (cols < ranks[b])
        gram = jnp.where(kept, grams[b], jnp.where(rows == cols, 1.0, 0.0))
        tiles.append([gram[8 * g : 8 * g + 8] for g in range(RANK // 8)])
    for k in range(RANK):
        first, at = k // 8, k % 8
        for b in range(blocks):
            tile = tiles[b]
            row = tile[first][at : at + 1, :]
            scaled = jnp.where(lane[:1] == k, 1.0, row) / row[:, k : k + 1]
            for g in range(first, RANK // 8):
                column = tile[g][:, k : k + 1]
                clear = lane == k
                if g == first:
                    column = jnp.where(sub[:, :1] > at, column, 0.0)
                    clear = clear & (sub > at)
                tile[g] = jnp.where(clear, 0.0, tile[g]) - column * scaled
    for b in range(blocks):
        done = jnp.concatenate(tiles[b], axis=0)
        pivots = jnp.sum(jnp.where(rows == cols, done, 0.0), axis=1, keepdims=True)
        lower = jnp.where(rows > cols, done, jnp.where(rows == cols, 1.0, 0.0))
        inverse = lax.dot_general(
            lower,
            lower / pivots,
            (((0,), (0,)), ((), ())),
            precision=HIGHEST,
            preferred_element_type=jnp.float32,
        )
        out_ref[b] = jnp.where(rows < ranks[b], inverse * (4.0 * math.sqrt(RANK)), 0.0)


def invert(place, block_ranks, packed):
    smem = pl.BlockSpec(memory_space=pltpu.SMEM)
    return pl.pallas_call(
        invert_kernel,
        out_shape=jax.ShapeDtypeStruct((2, RANK, RANK), jnp.float32),
        in_specs=[smem, smem, pl.BlockSpec(memory_space=pltpu.VMEM)],
        out_specs=pl.BlockSpec(memory_space=pltpu.VMEM),
        compiler_params=pltpu.CompilerParams(vmem_limit_bytes=16 * 2**20),
    )(place, block_ranks, packed)


def factor_of(factors_ref, level, slot, flipped=False):
    factor = factors_ref[level % 2, slot]
    if flipped:
        factor = jnp.concatenate([factor[:, RANK:], factor[:, :RANK]], axis=1)
    return factor


def joint(factors_ref, level, slot, other):
    return jnp.concatenate(
        [
            factor_of(factors_ref, level, slot),
            factor_of(factors_ref, level, other, True),
        ],
        axis=0,
    )


def matmul(left, right):
    return jnp.dot(left, right, preferred_element_type=jnp.float32)


def near_levels_kernel(base_ref, factors_ref, *rest):
    out_ref, mid_ref = rest[-2:]
    columns = out_ref.shape[2]
    for source, target, level, bit in ((base_ref, mid_ref, 0, 1), (mid_ref, out_ref, 1, 4)):
        for slot in range(SLOTS):
            other = slot ^ bit
            if slot < other:
                rows = jnp.concatenate([source[slot, :, :columns], source[other, :, :columns]], axis=0)
                mixed = matmul(joint(factors_ref, level, slot, other), rows)
                mixed = mixed.astype(jnp.bfloat16)
                target[slot] = mixed[:RANK]
                target[other] = mixed[RANK:]


def near_levels(base, factors, columns, *after):
    vmem = pl.BlockSpec(memory_space=pltpu.VMEM)
    shape = SLOTS, RANK, columns
    return pl.pallas_call(
        near_levels_kernel,
        out_shape=jax.ShapeDtypeStruct(shape, base.dtype),
        in_specs=[vmem, vmem] + [pl.BlockSpec(memory_space=pl.ANY)] * len(after),
        out_specs=vmem,
        scratch_shapes=[pltpu.VMEM(shape, base.dtype)],
        compiler_params=pltpu.CompilerParams(vmem_limit_bytes=16 * 2**20),
    )(base, factors, *[corner(other) for other in after])


def sums_of(factors_ref, level_ref, paired_ref, base_ref, slot, other):
    def third(at):
        rows = jnp.concatenate([level_ref[at], paired_ref[at]], axis=0)
        return matmul(factor_of(factors_ref, 2, at), rows).astype(jnp.bfloat16)

    columns = level_ref.shape[2]
    rows = jnp.concatenate([third(slot), third(other)], axis=0)
    bases = jnp.concatenate([base_ref[slot, :, :columns], base_ref[other, :, :columns]], axis=0)
    return lax.dot_general(
        rows, bases, (((1,), (1,)), ((), ())), preferred_element_type=jnp.float32
    )


PAIRS = tuple((slot, slot ^ 2) for slot in range(SLOTS) if slot < slot ^ 2)


def early_kernel(factors_ref, level_ref, paired_ref, base_ref, out_ref):
    for at, (slot, other) in enumerate(PAIRS):
        out_ref[at] = sums_of(factors_ref, level_ref, paired_ref, base_ref, slot, other)


def cross_kernel(factors_ref, level_ref, paired_ref, base_ref, early_ref, out_ref):
    for at, (slot, other) in enumerate(PAIRS):
        sums = early_ref[at] + sums_of(
            factors_ref, level_ref, paired_ref, base_ref, slot, other
        )
        parts = []
        for _ in range(3):
            part = sums.astype(jnp.bfloat16)
            parts.append(part)
            sums = sums - part.astype(jnp.float32)
        factor = (
            factor_of(factors_ref, 3, slot),
            factor_of(factors_ref, 3, other, True),
        )
        for side, block in enumerate((slot, other)):
            side_of = slice(side * RANK, (side + 1) * RANK)
            cross = matmul(factor[side], jnp.concatenate([part[:, side_of] for part in parts], axis=1))
            cross = cross[:, 2 * RANK :] + cross[:, RANK : 2 * RANK] + cross[:, :RANK]
            for x in range(4):
                out_ref[block // 4, x, block % 4] = cross[32 * x : 32 * x + 32]


def sums_call(kernel, shape, *arrays):
    vmem = pl.BlockSpec(memory_space=pltpu.VMEM)
    return pl.pallas_call(
        kernel,
        out_shape=jax.ShapeDtypeStruct(shape, jnp.float32),
        in_specs=[vmem] * len(arrays),
        out_specs=vmem,
        compiler_params=pltpu.CompilerParams(vmem_limit_bytes=16 * 2**20),
    )(*arrays)


def nothing_kernel(*refs):
    del refs


def corner(value):
    value = value.reshape(-1, *value.shape[-2:])
    return value[0, :16, :RANK]


def once_done(value, *others):
    others = [corner(other) for other in others]
    return pl.pallas_call(
        nothing_kernel,
        out_shape=jax.ShapeDtypeStruct(value.shape, value.dtype),
        in_specs=[pl.BlockSpec(memory_space=pl.ANY)] * (1 + len(others)),
        out_specs=pl.BlockSpec(memory_space=pl.ANY),
        input_output_aliases={0: 0},
    )(value, *others)


def exchange(blocks, axes):
    return lax.all_to_all(blocks, axes, 0, 0, tiled=True)


def gather(block, axes):
    count = lax.axis_size(axes)
    return exchange(jnp.broadcast_to(block[None], (count,) + block.shape), axes)


def swap(block, axis, bit):
    return lax.ppermute(block, axis, [(i, i ^ bit) for i in range(lax.axis_size(axis))])


def along_x(block, *after):
    count = lax.axis_size("x")
    shift = lambda d: lax.ppermute(block, "x", [(i, (i - d) % count) for i in range(count)])
    own = once_done(block, *after) if after else block
    return jnp.stack([own] + [shift(d) for d in range(1, count)])


def part(blocks, at, count):
    return lax.dynamic_slice_in_dim(blocks, at * count, count, 0)


def grams(panels, late):
    zl_at = lax.axis_index("zl")
    packed, panels = local_grams(panels, late)
    total = part(packed, zl_at, 1)
    for other in range(1, 4):
        total = total + swap(part(packed, zl_at ^ other, 1), "zl", other)
    return total, panels


def by_place(every):
    x_at = lax.axis_index("x")
    return [lax.dynamic_index_in_dim(every, (x + 4 - x_at) % 4, 0, False) for x in range(4)]


def gather_halved(solved):
    blocks, rows, _ = solved.shape
    top = jnp.max(jnp.abs(solved), axis=2)
    power = jnp.clip(jnp.floor(jnp.log2(jnp.maximum(top, 1e-36))), -120.0, 120.0)
    values = (solved * jnp.exp2(-power)[:, :, None]).astype(jnp.float16).reshape(-1, 8, RANK)
    powers = power.astype(jnp.float16).reshape(1, 1, blocks * rows)
    powers = jnp.pad(powers, ((0, 0), (0, 7), (0, RANK - blocks * rows)))
    sent = gather(jnp.concatenate([values, powers], axis=0), COL)
    power = sent[:, -1, 0, : blocks * rows].astype(jnp.float32).reshape(-1, blocks, rows)
    values = sent[:, :-1].astype(jnp.float32).reshape(-1, blocks, rows, RANK)
    values = values * jnp.exp2(power)[:, :, :, None]
    values = values.reshape(4, 2, 2, blocks, rows, RANK)
    return values.transpose(1, 3, 0, 2, 4, 5).reshape(-1, RANK)


def first_kernel(place_ref, mask_ref, panels_ref, own_ref, paired_ref, out_ref):
    columns = panels_ref.shape[1]
    half = RANK // 2
    for slot in range(SLOTS):
        mask = mask_ref[lax.shift_right_logical(place_ref[0], 1), slot].astype(jnp.float32)
        out_ref[slot, :, :columns] = panels_ref[slot * RANK : (slot + 1) * RANK]
        out_ref[slot, :half, columns:] = own_ref[0, slot, 0]
        paired = paired_ref[0, slot, 0].astype(jnp.float32) * mask
        out_ref[slot, half:, columns:] = paired.astype(jnp.bfloat16)


def first_part(place, panels, self_factors, partner_factors, link_mask, columns):
    half = RANK // 2
    spec = pl.BlockSpec(
        (1, SLOTS, 1, half, RANK),
        lambda i, place: (lax.shift_right_logical(place[0], 1), 0, place[0] & 1, 0, 0),
    )
    shape = SLOTS, RANK, columns + RANK
    split = LEVELS, SLOTS, 2, half, RANK
    return pl.pallas_call(
        first_kernel,
        out_shape=jax.ShapeDtypeStruct(shape, panels.dtype),
        grid_spec=pltpu.PrefetchScalarGridSpec(
            num_scalar_prefetch=1,
            grid=(1,),
            in_specs=[
                pl.BlockSpec(memory_space=pltpu.SMEM),
                pl.BlockSpec((panels.shape[0], columns), lambda i, place: (0, 0)),
                spec,
                spec,
            ],
            out_specs=pl.BlockSpec(shape, lambda i, place: (0, 0, 0)),
        ),
        compiler_params=pltpu.CompilerParams(vmem_limit_bytes=60 * 2**20),
    )(place, link_mask, panels, self_factors.reshape(split), partner_factors.reshape(split))


def body(panels, self_factors, partner_factors, link_mask, block_ranks):
    columns = panels.shape[1]
    early = columns // 8
    late = columns - early
    half = RANK // 2
    zl_at = lax.axis_index("zl")
    odd = zl_at % 2
    place = (lax.axis_index("x") * 2 + odd).astype(jnp.int32).reshape(1)

    first = first_part(place, panels, self_factors, partner_factors, link_mask, early)
    first = exchange(first, PEERS)
    own_half = first[:, :, early:]
    other_half = swap(own_half, "zl", 1)
    gram, panels = grams(panels, late)
    second = once_done(panels, other_half, gram).reshape(SLOTS, RANK, late)
    second = exchange(second, PEERS)

    gram = gram + swap(gram, "x", 1)
    gram = gram + swap(gram, "x", 2)
    inverse = invert(zl_at.astype(jnp.int32).reshape(1), block_ranks, gram)
    low, high = (jnp.where(odd == at, own_half, other_half) for at in range(2))
    factors = [jnp.concatenate([low[:, i], high[:, i]], axis=1) for i in (slice(half), slice(half, RANK))]
    factors = by_place(along_x(jnp.concatenate(factors, axis=2), inverse))
    lower, upper = jnp.stack(factors[:2]), jnp.stack(factors[2:])

    level = near_levels(first, lower, early)
    paired = swap(level, "core", 1)
    shape = len(PAIRS), 2 * RANK, 2 * RANK
    sums = sums_call(early_kernel, shape, upper, level, paired, first)
    level = near_levels(second, lower, late, sums)
    paired = swap(level, "core", 1)
    cross = sums_call(cross_kernel, (2, 4, 4, 32, RANK), upper, level, paired, second, sums)

    cross = exchange(cross.reshape(2 * 4, 4, 32, RANK), ("yl", "x"))
    cross = cross.reshape(2, 4, 4, 2, 16, RANK)
    cross = jnp.stack([cross[0].sum(0), cross[1].sum(0)], axis=1).reshape(16, 16, RANK)
    cross = exchange(cross, ("zh", "zl")).reshape(4, 4, 16, RANK).sum(1)
    pairs = jnp.stack([inverse, swap(inverse, "zl", 1)])
    pairs = [lax.dynamic_index_in_dim(pairs, zl_at % 2 ^ p, 0, False) for p in range(2)]
    inverse = jnp.concatenate(pairs, axis=0)
    solved = jnp.einsum("jrk,jkm->jrm", cross, inverse, precision=HIGHEST)
    return gather_halved(solved)


def solution(mesh):
    split = Mesh(mesh.devices.reshape(2, 2, 4, 2, 4, 4), ROW + COL)
    return jax.shard_map(
        body,
        mesh=split,
        in_specs=(P(ROW, COL), P(None, ROW, None), P(None, ROW, None), P(None, ROW), P(ROW)),
        out_specs=P(ROW, None),
        check_vma=False,
    )
```
